128 devices in a mesh: ctx: 16 (over z, y), head: 8 (over x, core).
Axes of the slice: x: 4, y: 4, z: 4, core: 2. Of those that a mesh axis runs over, the one named last changes fastest.
Arguments:
- tokens: bfloat16 [4096, 5120], P('ctx', 'head'), may hold values from -6 to 6
- gain: float32 [5120], P('head'), may hold values from 0.1 to 1.9
- qkv_weight: bfloat16 [5120, 7168], P('head')
- target: bfloat16 [4096, 5120], P('ctx', 'head'), may hold values from -6 to 6
- advantage: int32 [4096], P('ctx'), may hold values from -4 to 4
- segment: int32 [4096], P('ctx'), may hold values from 0 to 7, never falling along the last dimension, each value on 1 to 2048 neighbouring positions
Outputs:
- attn: bfloat16 [4096, 5120], P('ctx', 'head')
- grad_tokens: bfloat16 [4096, 5120], P('ctx', 'head')
- grad_gain: float32 [5120], P('head')
The draws below stay inside these ranges and needn't reach their ends.
Inputs may be any that keep to these rules, and one draw needn't show every extreme that they name: segment ids never fall along the tokens; each of the 8 rollouts has 1 to 2048 tokens, one exactly 2048.
All inputs are finite; a program needn't handle non-finite values.
Results may differ from the reference program's by a relative error of at most 0.015.
Values may be sent and summed in bfloat16 or wider, within the bound.
A program may use at most 128 MiB of HBM per device.

```python
import math
import jax
import jax.numpy as jnp
import numpy as np
from jax import lax

D = 5120
QH = 40
KVH = 8
HD = 128
SEQS = 8
TOKENS = 4096
LONGEST = 2048


def draw_qkv_weight(key, part):
    key = jax.random.fold_in(key, 11)
    per_group = QH // KVH
    weights = jax.random.normal(key, (D, KVH, per_group + 2, HD), jnp.float32) / jnp.sqrt(jnp.float32(D))
    return weights.reshape(D, KVH * (per_group + 2) * HD).astype(jnp.bfloat16)


def place_ends(result, stream_key, low, top_value):
    shape = result.shape
    index_at = [jax.random.randint(jax.random.fold_in(stream_key, axis), (), 0, shape[axis]) for axis in range(len(shape))]
    result = result.at[tuple(index_at)].set(low)
    longest = shape.index(max(shape))
    index_at[longest] = (index_at[longest] + 1) % shape[longest]
    return result.at[tuple(index_at)].set(top_value)


def block_levels(key, dims, cuts, smallest, high):
    loudness, own = 1.0, jax.random.fold_in(key, 6)
    for axis_at, parts in cuts:
        draws = jnp.exp(jax.random.uniform(jax.random.fold_in(own, axis_at), (parts,), jnp.float32, smallest / len(cuts), high / len(cuts)))
        loudness = loudness * jnp.repeat(draws, dims[axis_at] // parts).reshape([-1 if axis == axis_at else 1 for axis in range(len(dims))])
    return loudness


def length_profile(number_of, total, reach, slope):
    portions = [(1 << 20) // math.isqrt(rank ** slope) + 1 for rank in range(2, number_of + 1)]
    spare, holding = total - reach - (number_of - 1), [1] * (number_of - 1)
    while spare > 0:
        candidates = [i for i in range(number_of - 1) if holding[i] < reach]
        pool, left = sum([portions[i] for i in candidates]), spare
        for i in candidates:
            addition = min(reach - holding[i], max(1, left * portions[i] // pool), spare)
            holding[i] = holding[i] + addition
            spare = spare - addition
    return np.array([reach] + holding)


def ragged(rng, number_of, total, most, lean):
    if number_of == 2:
        one = jax.random.randint(rng, (), max(1, total - most), min(most, total - 1) + 1)
        return jnp.stack([one, total - one])
    tallies = jnp.asarray(length_profile(number_of, total, most, lean), jnp.int32)
    couples = (number_of - 1) // 2
    source_of, taker = tallies[1:1 + 2 * couples:2], tallies[2:2 + 2 * couples:2]
    slack = jnp.minimum(source_of - 1, most - taker)
    moved = jax.random.randint(jax.random.fold_in(rng, 1), (couples,), 0, 1 << 20) % (slack + 1)
    tallies = tallies.at[1:1 + 2 * couples:2].set(source_of - moved).at[2:2 + 2 * couples:2].set(taker + moved)
    return tallies[jax.random.permutation(jax.random.fold_in(rng, 2), number_of)]


def bell_draw(stream_key, extent, spread, most, split=(), held_as=jnp.bfloat16):
    loudness = block_levels(stream_key, extent, split, -0.22, 0.18) if split else 1.0
    result = jax.random.normal(stream_key, extent, jnp.float32) * spread * loudness
    return jnp.minimum(jnp.maximum(result, -most), most).astype(held_as)


def setup_inputs(seed: int = 0) -> dict:
    splits = jax.random.split(jax.random.key(seed), 7)
    return {
        "tokens": bell_draw(splits[0], (TOKENS, D), 1.0, 6.0, ((0, 16), (1, 8))),
        "gain": jnp.clip(1.0 + 0.18 * jax.random.normal(splits[1], (D,), jnp.float32), 0.1, 1.9),
        "qkv_weight": draw_qkv_weight(jax.random.fold_in(splits[6], 71), 0),
        "target": bell_draw(splits[3], (TOKENS, QH * HD), 1.0, 6.0, ((0, 16), (1, 8))),
        "advantage": place_ends(jax.random.randint(splits[4], (TOKENS,), -4, 5), jax.random.fold_in(splits[4], 1), -4, 4).astype(jnp.int32),
        "segment": jnp.searchsorted(jnp.cumsum(ragged(splits[5], SEQS, TOKENS, LONGEST, 1)), jnp.arange(TOKENS), side="right").astype(jnp.int32),
    }


epsilon = 1e-06

def reference(tokens, gain, qkv_weight, target, advantage, segment):
    features = tokens.astype(jnp.float32)
    recip = lax.rsqrt(lax.optimization_barrier(jnp.mean(features * features, -1, keepdims=True)) + epsilon)
    normed = (features * recip * gain).astype(jnp.bfloat16)
    proj = jnp.dot(normed, qkv_weight, preferred_element_type=jnp.float32).astype(jnp.bfloat16)
    token_count = proj.shape[0]
    per_group = QH // KVH
    proj = proj.reshape(token_count, KVH, per_group + 2, HD)
    queries = proj[:, :, :per_group]
    pairs = proj[:, :, per_group:]
    gradout = (0.25 * advantage.astype(jnp.float32)[:, None] * target.astype(jnp.float32)).astype(jnp.bfloat16)
    gradout = gradout.reshape(token_count, KVH, per_group, HD)
    positions = jnp.arange(token_count, dtype=jnp.int32)
    visible = (segment[:, None] == segment[None, :]) & (positions[None, :] <= positions[:, None])
    scale = HD ** (-0.5)

    def one_head(head_index):
        group = head_index // per_group
        member = head_index % per_group
        query_h = queries[:, group, member]
        key_h = pairs[:, group, 0]
        value_h = pairs[:, group, 1]
        grad_h = gradout[:, group, member]
        scores = jnp.dot(query_h, key_h.T, preferred_element_type=jnp.float32) * scale
        row_max = lax.optimization_barrier(jnp.max(jnp.where(visible, scores, -1e+30), -1, keepdims=True))
        total = lax.optimization_barrier(jnp.sum(jnp.where(visible, jnp.exp(scores - row_max), 0.0), -1, keepdims=True))
        lse = row_max + jnp.log(total)
        probs = jnp.where(visible, jnp.exp(scores - lse), 0.0)
        probs_b = probs.astype(jnp.bfloat16)
        output = jnp.dot(probs_b, value_h, preferred_element_type=jnp.float32).astype(jnp.bfloat16)
        delta = lax.optimization_barrier(jnp.sum(grad_h.astype(jnp.float32) * output.astype(jnp.float32), -1, keepdims=True))
        dprobs = jnp.dot(grad_h, value_h.T, preferred_element_type=jnp.float32)
        dscores = (probs * (dprobs - delta) * scale).astype(jnp.bfloat16)
        dquery = jnp.dot(dscores, key_h, preferred_element_type=jnp.float32).astype(jnp.bfloat16)
        dkey = jnp.dot(dscores.T, query_h, preferred_element_type=jnp.float32)
        dvalue = jnp.dot(probs_b.T, grad_h, preferred_element_type=jnp.float32)
        return (output, dquery, dkey, dvalue)
    output, dquery, dkey, dvalue = lax.map(one_head, jnp.arange(QH, dtype=jnp.int32))
    attn = output.transpose(1, 0, 2).reshape(token_count, QH * HD)
    dkey = lax.optimization_barrier(jnp.sum(dkey.reshape(KVH, per_group, token_count, HD), 1)).astype(jnp.bfloat16)
    dvalue = lax.optimization_barrier(jnp.sum(dvalue.reshape(KVH, per_group, token_count, HD), 1)).astype(jnp.bfloat16)
    dquery = dquery.reshape(KVH, per_group, token_count, HD).transpose(2, 0, 1, 3)
    dproj = jnp.concatenate([dquery, dkey.transpose(1, 0, 2)[:, :, None], dvalue.transpose(1, 0, 2)[:, :, None]], axis=2)
    dproj = dproj.reshape(token_count, KVH * (per_group + 2) * HD)
    dnormed = jnp.dot(dproj, qkv_weight.T, preferred_element_type=jnp.float32)
    grad_gain = lax.optimization_barrier(jnp.sum(dnormed * features * recip, 0))
    scaled = dnormed * gain
    inner = lax.optimization_barrier(jnp.sum(scaled * features, -1, keepdims=True))
    grad_tokens = (recip * scaled - features * recip ** 3 * inner / D).astype(jnp.bfloat16)
    return (attn, grad_tokens, grad_gain)
```

```python
import functools

import jax
import jax.numpy as jnp
from jax import lax
from jax.experimental import pallas as pl
from jax.experimental.pallas import tpu as pltpu
from jax.sharding import PartitionSpec as P

D = 5120
HD = 128
HEADS = 5
WINDOW = 8
EPSILON = 1e-06
SCALE = HD**-0.5
LOG2E = 1.4426950408889634
EXP_SCALE = SCALE * LOG2E
HIDDEN = -1e30
PIECES = ((640, 256), (0, 256), (256, 256), (512, 128))
STEPS = (2, 1, 3, 0)
F32 = jnp.float32
BF16 = jnp.bfloat16


def kernel(
    n_ctx, tok, gain, w_hbm, target, advantage, segment,
    attn, grad_tokens, grad_gain,
    xb, wv, part_send, part_recv, chip_sum, hold, own, relay, landed,
    stats, recip, seg_win, key_win, value_win, key_t, value_t, bias,
    q_rows, q_t, go_t, scores, expo, out_t, gp_rows, gp_t, dq_t, pair_acc, pair_send, pair_recv,
    dproj, inner_stats, dnormed, gain_stats,
    w_sem, ps_send, ps_recv, r1_send, r1_recv, r2_send, r2_recv, st_send, st_recv,
    seg_send, seg_recv, k_send, k_recv, v_send, v_recv, pair_ssem, pair_rsem,
    ag_send, ag_recv, in_send, in_recv, gg_send, gg_recv,
):
    rows = tok.shape[0]
    half = rows // 2
    c = lax.axis_index("ctx")
    h = lax.axis_index("head")
    x = h // 2
    p = lax.rem(h, 2)

    def head_of(xx, pp):
        return lax.rem(xx + 8, 4) * 2 + pp

    right, left, partner = head_of(x + 1, p), head_of(x - 1, p), head_of(x, 1 - p)
    started = []

    def remote(src, dst, send, recv, **where):
        axis, index = next(iter(where.items()))
        return pltpu.make_async_remote_copy(
            src_ref=src, dst_ref=dst, send_sem=send, recv_sem=recv,
            device_id={axis: index}, device_id_type=pl.DeviceIdType.MESH,
        )

    def start(copy, when=None):
        started.append((copy, when))
        if when is None:
            copy.start()
        else:
            pl.when(when)(copy.start)

    def arrived(dst, recv):
        remote(dst, dst, recv, recv, head=partner).wait_recv()

    barrier = pltpu.get_barrier_semaphore()
    for d in range(1, 8):
        pl.semaphore_signal(
            barrier, inc=1, device_id={"head": lax.rem(h + d, 8)}, device_id_type=pl.DeviceIdType.MESH
        )
    for d in range(1, n_ctx):
        pl.semaphore_signal(
            barrier, inc=1, device_id={"ctx": lax.rem(c + d, n_ctx)}, device_id_type=pl.DeviceIdType.MESH
        )

    def fetch(s, i):
        off, wide = PIECES[s]
        g = head_of(x + STEPS[i % 4], (1 - p) if i < 4 else p)
        first = pl.multiple_of(g * 896 + off, 128)
        return g, pltpu.make_async_copy(
            w_hbm.at[:, pl.ds(first, wide)], wv.at[g, :, pl.ds(off, wide)], w_sem.at[s, i]
        )

    for s in range(4):
        for i in range(8):
            fetch(s, i)[1].start()

    features = tok[...].astype(F32)
    xb[...] = (features * gain[...]).astype(BF16)
    stats[h] = lax.dot_general(
        jnp.ones((8, tok.shape[1]), F32), features * features, (((1,), (1,)), ((), ())),
        precision=lax.Precision.HIGHEST, preferred_element_type=F32,
    )
    seg_win[0] = jnp.broadcast_to(segment[...].astype(F32), (16, rows)).astype(BF16)

    pl.semaphore_wait(barrier, 7 + n_ctx - 1)

    def project(s):
        off, wide = PIECES[s]
        cols = pl.ds(off, wide)
        for i in range(4):
            g, copy = fetch(s, i)
            copy.wait()
            part_send[i, :, off : off + wide] = jnp.dot(
                xb[...], wv[g, :, off : off + wide], preferred_element_type=F32
            ).astype(BF16)
            start(remote(
                part_send.at[i, :, cols], part_recv.at[i, :, cols],
                ps_send.at[s, i], ps_recv.at[s, i], head=partner,
            ))
        for i in range(4):
            g, copy = fetch(s, 4 + i)
            copy.wait()
            mine = jnp.dot(xb[...], wv[g, :, off : off + wide], preferred_element_type=F32)
            arrived(part_recv.at[i, :, cols], ps_recv.at[s, i])
            mine = mine + part_recv[i, :, off : off + wide].astype(F32)
            if i < 3:
                chip_sum[i, :, off : off + wide] = mine.astype(BF16)
            top = pl.ds(0, half)
            low = pl.ds(half, half)
            if i == 0:
                start(remote(
                    chip_sum.at[0, top, cols], relay.at[0, :, cols],
                    r1_send.at[s, 0], r1_recv.at[s, 0], head=right,
                ))
                start(remote(
                    chip_sum.at[0, low, cols], relay.at[1, :, cols],
                    r1_send.at[s, 1], r1_recv.at[s, 1], head=left,
                ))
            elif i == 1:
                hold[0, :, off : off + wide] = mine[:half]
                start(remote(
                    chip_sum.at[1, low, cols], landed.at[0, low, cols],
                    r2_send.at[s, 0], r2_recv.at[s, 0], head=right,
                ))
            elif i == 2:
                hold[1, :, off : off + wide] = mine[half:]
                start(remote(
                    chip_sum.at[2, top, cols], landed.at[1, top, cols],
                    r2_send.at[s, 1], r2_recv.at[s, 1], head=left,
                ))
            else:
                own[:, off : off + wide] = mine

    def pass_on(s):
        off, wide = PIECES[s]
        cols = pl.ds(off, wide)
        top = pl.ds(0, half)
        low = pl.ds(half, half)
        arrived(relay.at[0, :, cols], r1_recv.at[s, 0])
        chip_sum[1, :half, off : off + wide] = (
            hold[0, :, off : off + wide] + relay[0, :, off : off + wide].astype(F32)
        ).astype(BF16)
        start(remote(
            chip_sum.at[1, top, cols], landed.at[0, top, cols],
            r2_send.at[s, 2], r2_recv.at[s, 2], head=right,
        ))
        arrived(relay.at[1, :, cols], r1_recv.at[s, 1])
        chip_sum[2, half:, off : off + wide] = (
            hold[1, :, off : off + wide] + relay[1, :, off : off + wide].astype(F32)
        ).astype(BF16)
        start(remote(
            chip_sum.at[2, low, cols], landed.at[1, low, cols],
            r2_send.at[s, 3], r2_recv.at[s, 3], head=left,
        ))

    def finish(s):
        off, wide = PIECES[s]
        cols = pl.ds(off, wide)
        top = pl.ds(0, half)
        low = pl.ds(half, half)
        arrived(landed.at[0, low, cols], r2_recv.at[s, 0])
        arrived(landed.at[1, top, cols], r2_recv.at[s, 1])
        arrived(landed.at[0, top, cols], r2_recv.at[s, 2])
        arrived(landed.at[1, low, cols], r2_recv.at[s, 3])
        total = own[:, off : off + wide] + landed[0, :, off : off + wide].astype(F32)
        total = total + landed[1, :, off : off + wide].astype(F32)
        scale = recip[:, :1]
        return (total * scale).astype(BF16)

    project(0)
    for d in range(1, 8):
        start(remote(
            stats.at[h], stats.at[h], st_send.at[d], st_recv.at[h], head=lax.rem(h + d, 8),
        ))
    for j in range(1, WINDOW + 1):
        start(remote(
            seg_win.at[0], seg_win.at[j], seg_send.at[j], seg_recv.at[j],
            ctx=jnp.minimum(c + j, n_ctx - 1),
        ), c + j < n_ctx)
    pass_on(0)
    project(1)
    for d in range(1, 8):
        sender = lax.rem(h + d, 8)
        arrived(stats.at[sender], st_recv.at[sender])
    squares = jnp.sum(stats[...], 0)
    recip[...] = jnp.broadcast_to(
        lax.rsqrt(jnp.transpose(squares)[:, :1] / D + EPSILON), (rows, HD)
    )

    pair = finish(0)
    key_win[0] = pair[:, :HD]
    value_win[0] = pair[:, HD:]
    for j in range(1, WINDOW + 1):
        later = jnp.minimum(c + j, n_ctx - 1)
        start(remote(key_win.at[0], key_win.at[j], k_send.at[j], k_recv.at[j], ctx=later), c + j < n_ctx)
        start(remote(value_win.at[0], value_win.at[j], v_send.at[j], v_recv.at[j], ctx=later), c + j < n_ctx)

    pass_on(1)
    project(2)
    pass_on(2)
    project(3)
    pass_on(3)

    factor = 0.25 * advantage[...].astype(F32)
    for r in range(HEADS):
        block = jnp.transpose(target[:, r * HD : (r + 1) * HD].astype(F32))
        go_t[:, r * rows : (r + 1) * rows] = (block * factor).astype(BF16)

    def queries(s):
        q = finish(s)
        first = PIECES[s][0] // HD
        for i in range(PIECES[s][1] // HD):
            one = q[:, i * HD : (i + 1) * HD]
            q_rows[(first + i) * rows : (first + i + 1) * rows] = one
            q_t[:, (first + i) * rows : (first + i + 1) * rows] = jnp.transpose(one.astype(F32)).astype(BF16)

    queries(1)

    blocks = jnp.minimum(c, WINDOW) + 1
    q_seg = seg_win[0, :1].astype(F32)

    def prepare(j, diagonal):
        key_t[j] = jnp.transpose(key_win[j].astype(F32)).astype(BF16)
        value_t[j] = jnp.transpose(value_win[j].astype(F32)).astype(BF16)
        k_seg = jnp.transpose(seg_win[j].astype(F32))[:, :1]
        visible = k_seg == q_seg
        if diagonal:
            k_pos = lax.broadcasted_iota(jnp.int32, (rows, rows), 0)
            q_pos = lax.broadcasted_iota(jnp.int32, (rows, rows), 1)
            visible = visible & (k_pos <= q_pos)
        bias[j] = jnp.where(visible, 0.0, HIDDEN)

    prepare(0, True)

    @pl.loop(1, blocks)
    def _(j):
        arrived(seg_win.at[j], seg_recv.at[j])
        arrived(key_win.at[j], k_recv.at[j])
        arrived(value_win.at[j], v_recv.at[j])
        prepare(j, False)

    def attend(s, fresh):
        off, wide = PIECES[s]
        heads = wide // HD
        n = heads * rows
        first = off // HD * rows
        span = slice(first, first + n)

        def score_block(j, top):
            block = jnp.dot(key_win[j], q_t[:, span], preferred_element_type=F32)
            block = block + jnp.concatenate([bias[j]] * heads, axis=1)
            scores[j, :, :n] = block
            return jnp.maximum(top, jnp.max(block.reshape(rows // 8, 8, n), 0))

        top = lax.fori_loop(0, blocks, score_block, jnp.full((8, n), HIDDEN, F32))
        top = jnp.max(top, 0, keepdims=True) * EXP_SCALE
        out_t[:, :n] = jnp.zeros((HD, n), F32)

        def expo_block(j, total):
            e = jnp.exp2(scores[j, :, :n] * EXP_SCALE - top)
            eb = e.astype(BF16)
            expo[j, :, :n] = eb
            out_t[:, :n] += jnp.dot(value_t[j], eb, preferred_element_type=F32)
            return total + jnp.sum(e.reshape(rows // 8, 8, n), 0)

        total = lax.fori_loop(0, blocks, expo_block, jnp.zeros((8, n), F32))
        inverse = 1.0 / jnp.sum(total, 0, keepdims=True)
        out_b = (out_t[:, :n] * inverse).astype(BF16).astype(F32)
        go = go_t[:, span].astype(F32)
        delta = jnp.sum(go * out_b, 0, keepdims=True) * inverse
        scaled = go * inverse
        gp_t[:, :n] = scaled.astype(BF16)
        for i in range(heads):
            r = off // HD + i
            attn[:, r * HD : (r + 1) * HD] = jnp.transpose(out_b[:, i * rows : (i + 1) * rows]).astype(BF16)
            gp_rows[i * rows : (i + 1) * rows] = jnp.transpose(scaled[:, i * rows : (i + 1) * rows]).astype(BF16)
        dq_t[:, :n] = jnp.zeros((HD, n), F32)

        @pl.loop(0, blocks)
        def _(j):
            dp = jnp.dot(value_win[j], gp_t[:, :n], preferred_element_type=F32)
            eb = expo[j, :, :n]
            ds = (eb.astype(F32) * (dp - delta)).astype(BF16)
            dk = jnp.dot(ds, q_rows[span], preferred_element_type=F32)
            dv = jnp.dot(eb, gp_rows[:n], preferred_element_type=F32)
            if fresh:
                pair_acc[j, :, :HD] = dk
                pair_acc[j, :, HD:] = dv
            else:
                pair_acc[j, :, :HD] += dk
                pair_acc[j, :, HD:] += dv
            dq_t[:, :n] += jnp.dot(key_t[j], ds, preferred_element_type=F32)

        inner = jnp.zeros((1, rows), F32)
        for i in range(heads):
            r = off // HD + i
            one = dq_t[:, i * rows : (i + 1) * rows] * SCALE
            dproj[h, :, r * HD : (r + 1) * HD] = jnp.transpose(one).astype(BF16)
            inner += jnp.sum(one * q_t[:, r * rows : (r + 1) * rows].astype(F32), 0, keepdims=True)
        return inner

    def slot(ref, s, who, lo, size):
        off, wide = PIECES[s]
        return ref.at[who, pl.ds(lo, size), pl.ds(off, wide)]

    def move(s, n, who, lo, size, to):
        start(remote(slot(dproj, s, who, lo, size), slot(dproj, s, who, lo, size),
                     ag_send.at[s, n], ag_recv.at[s, n], head=to))

    def landed_piece(s, n, who, lo, size):
        arrived(slot(dproj, s, who, lo, size), ag_recv.at[s, n])

    far = head_of(x + 2, p)

    def gather_send(s):
        move(s, 0, h, 0, rows, right)
        move(s, 1, h, 0, rows, left)
        move(s, 2, h, 0, rows, partner)

    def gather_pass(s):
        landed_piece(s, 0, left, 0, rows)
        move(s, 3, left, 0, half, right)
        move(s, 5, left, 0, rows, partner)
        landed_piece(s, 1, right, 0, rows)
        move(s, 4, right, half, half, left)
        move(s, 6, right, 0, rows, partner)

    def gather_far(s):
        landed_piece(s, 3, far, 0, half)
        move(s, 7, far, 0, half, partner)
        landed_piece(s, 4, far, half, half)
        move(s, 8, far, half, half, partner)

    def add(s, who, fresh=False):
        off, wide = PIECES[s]
        value = lax.dot_general(
            dproj[who, :, off : off + wide], wv[who, :, off : off + wide],
            (((1,), (1,)), ((), ())), preferred_element_type=F32,
        )
        if fresh:
            dnormed[...] = value
        else:
            dnormed[...] += value

    def add_own(s, fresh=False):
        add(s, h, fresh)
        add(s, left)
        add(s, right)

    def add_rest(s):
        add(s, far)
        landed_piece(s, 2, partner, 0, rows)
        add(s, partner)
        landed_piece(s, 5, head_of(x - 1, 1 - p), 0, rows)
        add(s, head_of(x - 1, 1 - p))
        landed_piece(s, 6, head_of(x + 1, 1 - p), 0, rows)
        add(s, head_of(x + 1, 1 - p))
        other = head_of(x + 2, 1 - p)
        landed_piece(s, 7, other, 0, half)
        landed_piece(s, 8, other, half, half)
        add(s, other)

    inner = attend(1, True)
    gather_send(1)
    queries(2)
    inner += attend(2, False)
    gather_pass(1)
    gather_send(2)
    queries(3)
    inner += attend(3, False)
    gather_far(1)
    gather_pass(2)
    gather_send(3)

    for j in range(WINDOW, 0, -1):
        earlier = jnp.maximum(c - j, 0)

        def send_pair(j=j):
            pair_send[j, :, :HD] = (pair_acc[j, :, :HD] * SCALE).astype(BF16)
            pair_send[j, :, HD:] = pair_acc[j, :, HD:].astype(BF16)

        pl.when(c >= j)(send_pair)
        start(remote(
            pair_send.at[j], pair_recv.at[j], pair_ssem.at[j], pair_rsem.at[j], ctx=earlier,
        ), c >= j)

    add_own(1, True)
    gather_far(2)
    gather_pass(3)
    add_rest(1)
    add_own(2)
    gather_far(3)
    add_rest(2)
    add_own(3)
    add_rest(3)

    pair_acc[0, :, :HD] = pair_acc[0, :, :HD] * SCALE

    @pl.loop(1, jnp.minimum(n_ctx - 1 - c, WINDOW) + 1)
    def _(j):
        arrived(pair_recv.at[j], pair_rsem.at[j])
        pair_acc[0] += pair_recv[j].astype(F32)

    pair_grad = pair_acc[0]
    dproj[h, :, PIECES[0][0] :] = pair_grad.astype(BF16)
    gather_send(0)
    prod = pair_grad[:, :HD] * key_win[0].astype(F32) + pair_grad[:, HD:] * value_win[0].astype(F32)
    inner += jnp.sum(jnp.transpose(prod), 0, keepdims=True)
    inner_stats[h] = jnp.broadcast_to(inner, (8, rows))
    for d in range(1, 8):
        start(remote(
            inner_stats.at[h], inner_stats.at[h], in_send.at[d], in_recv.at[h], head=lax.rem(h + d, 8),
        ))
    gather_pass(0)
    add_own(0)
    gather_far(0)
    for d in range(1, 8):
        sender = lax.rem(h + d, 8)
        arrived(inner_stats.at[sender], in_recv.at[sender])
    add_rest(0)

    scale = recip[:, :1]
    weighted = tok[...].astype(F32) * scale
    gain_part = jnp.sum(dnormed[...] * weighted, 0, keepdims=True)
    lanes = tok.shape[1] // 128
    gain_stats[c] = jnp.zeros((8, 128), F32)
    for k in range(lanes):
        gain_stats[c, k : k + 1] = gain_part[:, k * 128 : (k + 1) * 128]
    for d in range(1, n_ctx):
        start(remote(
            gain_stats.at[c], gain_stats.at[c], gg_send.at[d], gg_recv.at[c], ctx=lax.rem(c + d, n_ctx),
        ))
    inner_col = jnp.transpose(jnp.sum(inner_stats[...], 0))[:, :1]
    grad_tokens[...] = (
        dnormed[...] * gain[...] * scale - weighted * (scale * inner_col * (1.0 / D))
    ).astype(BF16)
    for d in range(1, n_ctx):
        sender = lax.rem(c + d, n_ctx)
        arrived(gain_stats.at[sender], gg_recv.at[sender])
    gain_total = jnp.sum(gain_stats[...], 0)
    for k in range(lanes):
        grad_gain[:, k * 128 : (k + 1) * 128] = gain_total[k : k + 1]

    for copy, when in started:
        if when is None:
            copy.wait_send()
        else:
            pl.when(when)(copy.wait_send)


def on_device(n_ctx, tokens, gain, qkv_weight, target, advantage, segment):
    rows, wide = tokens.shape
    group = qkv_weight.shape[1] // 8
    n = 2 * rows
    slots = WINDOW + 1
    vmem = pl.BlockSpec(memory_space=pltpu.VMEM)
    scratch = [
        ((rows, wide), BF16), ((8, wide, group), BF16),
        ((4, rows, group), BF16), ((4, rows, group), BF16), ((3, rows, group), BF16),
        ((2, rows // 2, group), F32), ((rows, group), F32),
        ((2, rows // 2, group), BF16), ((2, rows, group), BF16),
        ((8, 8, rows), F32), ((rows, HD), F32), ((slots, 16, rows), BF16),
        ((slots, rows, HD), BF16), ((slots, rows, HD), BF16),
        ((slots, HD, rows), BF16), ((slots, HD, rows), BF16), ((slots, rows, rows), F32),
        ((HEADS * rows, HD), BF16), ((HD, HEADS * rows), BF16), ((HD, HEADS * rows), BF16),
        ((slots, rows, n), F32), ((slots, rows, n), BF16), ((HD, n), F32),
        ((n, HD), BF16), ((HD, n), BF16), ((HD, n), F32),
        ((slots, rows, 2 * HD), F32), ((slots, rows, 2 * HD), BF16), ((slots, rows, 2 * HD), BF16),
        ((8, rows, group), BF16), ((8, 8, rows), F32), ((rows, wide), F32), ((n_ctx, 8, 128), F32),
    ]
    sems = [
        (4, 8), (4, 4), (4, 4), (4, 2), (4, 2), (4, 4), (4, 4), (8,), (8,),
        (slots,), (slots,), (slots,), (slots,), (slots,), (slots,), (slots,), (slots,),
        (4, 9), (4, 9), (8,), (8,), (n_ctx,), (n_ctx,),
    ]
    out, grad_tokens, grad_gain = pl.pallas_call(
        functools.partial(kernel, n_ctx),
        out_shape=(
            jax.ShapeDtypeStruct((rows, HEADS * HD), BF16),
            jax.ShapeDtypeStruct((rows, wide), BF16),
            jax.ShapeDtypeStruct((1, wide), F32),
        ),
        in_specs=[vmem, vmem, pl.BlockSpec(memory_space=pl.ANY), vmem, vmem, vmem],
        out_specs=(vmem, vmem, vmem),
        scratch_shapes=[pltpu.VMEM(shape, dtype) for shape, dtype in scratch]
        + [pltpu.SemaphoreType.DMA(shape) for shape in sems],
        compiler_params=pltpu.CompilerParams(
            collective_id=0, has_side_effects=True, vmem_limit_bytes=60 * 1024 * 1024
        ),
    )(
        tokens, gain.reshape(1, wide), qkv_weight, target,
        advantage.reshape(1, rows), segment.reshape(1, rows),
    )
    return out, grad_tokens, grad_gain.reshape(wide)


def solution(mesh):
    placed = (P("ctx", "head"), P("head"), P("head", None), P("ctx", "head"), P("ctx"), P("ctx"))
    return jax.shard_map(
        functools.partial(on_device, mesh.shape["ctx"]),
        mesh=mesh,
        in_specs=placed,
        out_specs=(P("ctx", "head"), P("ctx", "head"), P("head")),
        check_vma=False,
    )
```

```python
import functools

import jax
import jax.numpy as jnp
from jax import lax
from jax.experimental import pallas as pl
from jax.experimental.pallas import tpu as pltpu
from jax.sharding import PartitionSpec as P

D = 5120
HD = 128
HEADS = 5
WINDOW = 8
EPSILON = 1e-06
SCALE = HD**-0.5
LOG2E = 1.4426950408889634
EXP_SCALE = SCALE * LOG2E
HIDDEN = -1e30
PIECES = ((640, 256), (0, 256), (256, 384))
GROUP = 3
STEPS = (2, 1, 3, 0)
F32 = jnp.float32
BF16 = jnp.bfloat16


def kernel(
    n_ctx, tok, gain, w_hbm, target, advantage, segment,
    attn, grad_tokens, grad_gain,
    xb, wv, part_send, part_recv, chip_sum, hold, own, relay, landed, landed_far,
    stats, recip, window, key_t, value_t, bias,
    q_rows, q_t, go_t, scores, expo, out_t, gp_rows, gp_t, dq_t, pair_acc, pair_send, pair_recv,
    dproj, inner_stats, dnormed, gain_stats,
    w_sem, ps_send, ps_recv, r1_send, r1_recv, r2_send, r2_recv, st_send, st_recv,
    win_ssem, win_rsem, pair_ssem, pair_rsem,
    ag_send, ag_recv, in_send, in_recv, gg_send, gg_recv,
):
    rows, wide_in = tok.shape
    half = rows // 2
    seg_at = 2 * rows
    c = lax.axis_index("ctx")
    h = lax.axis_index("head")
    x = h // 2
    p = lax.rem(h, 2)
    z = c // 4
    y = lax.rem(c, 4)
    rings = n_ctx // 4
    up, down = z * 4 + lax.rem(y + 1, 4), z * 4 + lax.rem(y + 3, 4)

    def head_of(xx, pp):
        return lax.rem(xx + 8, 4) * 2 + pp

    right, left, partner = head_of(x + 1, p), head_of(x - 1, p), head_of(x, 1 - p)
    far = head_of(x + 2, p)
    started = []

    def remote(src, dst, send, recv, **where):
        axis, index = next(iter(where.items()))
        return pltpu.make_async_remote_copy(
            src_ref=src, dst_ref=dst, send_sem=send, recv_sem=recv,
            device_id={axis: index}, device_id_type=pl.DeviceIdType.MESH,
        )

    def start(copy, when=None):
        started.append((copy, when))
        if when is None:
            copy.start()
        else:
            pl.when(when)(copy.start)

    def arrived(dst, recv):
        remote(dst, dst, recv, recv, head=partner).wait_recv()

    barrier = pltpu.get_barrier_semaphore()
    for other in (partner, right, left, head_of(x + 2, p)):
        pl.semaphore_signal(
            barrier, inc=1, device_id={"head": other}, device_id_type=pl.DeviceIdType.MESH
        )
    others = [lax.rem(c + d, n_ctx) for d in range(1, n_ctx)]
    for other in others:
        pl.semaphore_signal(
            barrier, inc=1, device_id={"ctx": other}, device_id_type=pl.DeviceIdType.MESH
        )

    def fetch(s, i):
        off, wide = PIECES[s]
        g = head_of(x + STEPS[i % 4], (1 - p) if i < 4 else p)
        first = pl.multiple_of(g * 896 + off, 128)
        return g, pltpu.make_async_copy(
            w_hbm.at[:, pl.ds(first, wide)], wv.at[g, :, pl.ds(off, wide)], w_sem.at[s, i]
        )

    for s in range(3):
        for i in range(8):
            fetch(s, i)[1].start()

    gain_row = gain[...].reshape(1, wide_in)
    xb[...] = (tok[...].astype(F32) * gain_row).astype(BF16)

    def project(s):
        off, wide = PIECES[s]
        cols = pl.ds(off, wide)
        for i in range(4):
            g, copy = fetch(s, i)
            copy.wait()
            part_send[i, :, off : off + wide] = jnp.dot(
                xb[...], wv[g, :, off : off + wide], preferred_element_type=F32
            ).astype(BF16)
            if s == 0 and i == 0:
                pl.semaphore_wait(barrier, 4 + len(others))
            start(remote(
                part_send.at[i, :, cols], part_recv.at[i, :, cols],
                ps_send.at[s, i], ps_recv.at[s, i], head=partner,
            ))
        for i in range(4):
            g, copy = fetch(s, 4 + i)
            copy.wait()
            mine = jnp.dot(xb[...], wv[g, :, off : off + wide], preferred_element_type=F32)
            arrived(part_recv.at[i, :, cols], ps_recv.at[s, i])
            mine = mine + part_recv[i, :, off : off + wide].astype(F32)
            if i < 3:
                chip_sum[i, :, off : off + wide] = mine.astype(BF16)
            top = pl.ds(0, half)
            low = pl.ds(half, half)
            if s == 0 and i < 3:
                start(remote(
                    chip_sum.at[i, :, cols], (landed_far, landed.at[0, :, cols], landed.at[1, :, cols])[i],
                    r2_send.at[s, i], r2_recv.at[s, i], head=(far, right, left)[i],
                ))
            elif i == 0:
                start(remote(
                    chip_sum.at[0, top, cols], relay.at[0, :, cols],
                    r1_send.at[s, 0], r1_recv.at[s, 0], head=right,
                ))
                start(remote(
                    chip_sum.at[0, low, cols], relay.at[1, :, cols],
                    r1_send.at[s, 1], r1_recv.at[s, 1], head=left,
                ))
            elif i == 1:
                hold[0, :, off : off + wide] = mine[:half]
                start(remote(
                    chip_sum.at[1, low, cols], landed.at[0, low, cols],
                    r2_send.at[s, 0], r2_recv.at[s, 0], head=right,
                ))
            elif i == 2:
                hold[1, :, off : off + wide] = mine[half:]
                start(remote(
                    chip_sum.at[2, top, cols], landed.at[1, top, cols],
                    r2_send.at[s, 1], r2_recv.at[s, 1], head=left,
                ))
            else:
                own[:, off : off + wide] = mine

    def pass_on(s):
        off, wide = PIECES[s]
        cols = pl.ds(off, wide)
        top = pl.ds(0, half)
        low = pl.ds(half, half)
        arrived(relay.at[0, :, cols], r1_recv.at[s, 0])
        chip_sum[1, :half, off : off + wide] = (
            hold[0, :, off : off + wide] + relay[0, :, off : off + wide].astype(F32)
        ).astype(BF16)
        start(remote(
            chip_sum.at[1, top, cols], landed.at[0, top, cols],
            r2_send.at[s, 2], r2_recv.at[s, 2], head=right,
        ))
        arrived(relay.at[1, :, cols], r1_recv.at[s, 1])
        chip_sum[2, half:, off : off + wide] = (
            hold[1, :, off : off + wide] + relay[1, :, off : off + wide].astype(F32)
        ).astype(BF16)
        start(remote(
            chip_sum.at[2, low, cols], landed.at[1, low, cols],
            r2_send.at[s, 3], r2_recv.at[s, 3], head=left,
        ))

    def finish(s):
        off, wide = PIECES[s]
        cols = pl.ds(off, wide)
        top = pl.ds(0, half)
        low = pl.ds(half, half)
        if s == 0:
            arrived(landed_far, r2_recv.at[0, 0])
            arrived(landed.at[0, :, cols], r2_recv.at[0, 1])
            arrived(landed.at[1, :, cols], r2_recv.at[0, 2])
        else:
            arrived(landed.at[0, low, cols], r2_recv.at[s, 0])
            arrived(landed.at[1, top, cols], r2_recv.at[s, 1])
            arrived(landed.at[0, top, cols], r2_recv.at[s, 2])
            arrived(landed.at[1, low, cols], r2_recv.at[s, 3])
        total = own[:, off : off + wide] + landed[0, :, off : off + wide].astype(F32)
        total = total + landed[1, :, off : off + wide].astype(F32)
        if s == 0:
            total = total + landed_far[...].astype(F32)
        scale = recip[:, :1]
        return (total * scale).astype(BF16)

    def small_first(ref, send, recv):
        start(remote(ref.at[0], ref.at[1], send.at[0], recv.at[0], head=partner))

    def small_second(ref, send, recv):
        arrived(ref.at[1], recv.at[0])
        ref[2] = ref[0] + ref[1]
        for d in range(1, 4):
            start(remote(ref.at[2], ref.at[2 + d], send.at[d], recv.at[d], head=head_of(x + d, p)))

    def small_total(ref, recv):
        for d in range(1, 4):
            arrived(ref.at[2 + d], recv.at[d])
        return jnp.transpose(ref[2] + ref[3] + ref[4] + ref[5])[:, :1]

    project(0)
    features = tok[...].astype(F32)
    stats[0] = lax.dot_general(
        jnp.ones((8, wide_in), F32), features * features, (((1,), (1,)), ((), ())),
        precision=lax.Precision.HIGHEST, preferred_element_type=F32,
    )
    small_first(stats, st_send, st_recv)
    seg_row = segment[...].astype(F32)
    which = lax.broadcasted_iota(jnp.int32, (16, HD), 0)
    seg_block = jnp.zeros((16, HD), F32)
    for k in range(rows // HD):
        seg_block = jnp.where(which == k, seg_row[:, k * HD : (k + 1) * HD], seg_block)
    window[0, seg_at:] = seg_block.astype(BF16)
    small_second(stats, st_send, st_recv)
    project(1)
    recip[...] = jnp.broadcast_to(
        lax.rsqrt(small_total(stats, st_recv) / D + EPSILON), (rows, HD)
    )

    pair = finish(0)
    window[0, :rows] = pair[:, :HD]
    window[0, rows:seg_at] = pair[:, HD:]

    def share(n, src, dst, to, when):
        start(remote(window.at[src], window.at[dst], win_ssem.at[n], win_rsem.at[dst], ctx=to), when)

    def here(j):
        pl.when(c >= j)(lambda: arrived(window.at[j], win_rsem.at[j]))

    def share_first():
        for d in (1, 2):
            share(d, 0, 4 * d, jnp.minimum(c + 4 * d, n_ctx - 1), z + d < rings)
        for d in range(1, 4):
            share(2 + d, 0, d, z * 4 + jnp.minimum(y + d, 3), y + d <= 3)

    def share_second():
        here(4)
        for d in (1, 3, 2):
            share(5 + d, 4, 4 + d - 4 * ((y + d) // 4), z * 4 + lax.rem(y + d, 4), z >= 1)

    def share_third():
        here(8)
        for d in range(1, 4):
            share(8 + d, 8, 8 - d, z * 4 + jnp.maximum(y - d, 0), (z >= 2) & (y >= d))

    def share_last():
        for j in (1, 2, 3, 5, 6, 7):
            here(j)

    share_first()
    pass_on(1)
    project(2)
    share_second()
    pass_on(2)

    factor = 0.25 * advantage[...].astype(F32)
    for r in range(HEADS):
        block = jnp.transpose(target[:, r * HD : (r + 1) * HD].astype(F32))
        go_t[:, r * rows : (r + 1) * rows] = (block * factor).astype(BF16)

    def queries(s):
        q = finish(s)
        first = PIECES[s][0] // HD
        for i in range(PIECES[s][1] // HD):
            one = q[:, i * HD : (i + 1) * HD]
            q_rows[(first + i) * rows : (first + i + 1) * rows] = one
            q_t[:, (first + i) * rows : (first + i + 1) * rows] = jnp.transpose(one.astype(F32)).astype(BF16)

    share_third()
    queries(1)
    share_last()

    blocks = jnp.minimum(c, WINDOW) + 1
    groups = (blocks + GROUP - 1) // GROUP

    def prepare(j, diagonal):
        span = pl.ds(pl.multiple_of(j * rows, rows), rows)
        key_t[:, span] = jnp.transpose(window[j, :rows].astype(F32)).astype(BF16)
        value_t[:, span] = jnp.transpose(window[j, rows:seg_at].astype(F32)).astype(BF16)
        ids = jnp.transpose(window[j, seg_at:].astype(F32))
        for k in range(rows // HD):
            visible = ids[:, k : k + 1] == seg_row
            if diagonal:
                k_pos = lax.broadcasted_iota(jnp.int32, (HD, rows), 0) + k * HD
                q_pos = lax.broadcasted_iota(jnp.int32, (HD, rows), 1)
                visible = visible & (k_pos <= q_pos)
            bias[j, k * HD : (k + 1) * HD] = jnp.where(visible, 0.0, HIDDEN)

    prepare(0, True)

    @pl.loop(1, blocks)
    def _(j):
        prepare(j, False)

    @pl.loop(blocks, groups * GROUP)
    def _(j):
        span = pl.ds(pl.multiple_of(j * rows, rows), rows)
        window[j] = jnp.zeros((seg_at + 16, HD), BF16)
        key_t[:, span] = jnp.zeros((HD, rows), BF16)
        value_t[:, span] = jnp.zeros((HD, rows), BF16)
        bias[j] = jnp.full((rows, rows), HIDDEN, F32)

    def forward(s):
        off, wide = PIECES[s]
        heads = wide // HD
        n = heads * rows
        first = off // HD * rows
        span = slice(first, first + n)

        def score_group(g, top):
            for u in range(GROUP):
                j = g * GROUP + u
                block = jnp.dot(window[j, :rows], q_t[:, span], preferred_element_type=F32)
                block = block + jnp.concatenate([bias[j]] * heads, axis=1)
                scores[j, :, :n] = block
                top = jnp.maximum(top, jnp.max(block.reshape(rows // 8, 8, n), 0))
            return top

        top = lax.fori_loop(0, groups, score_group, jnp.full((8, n), HIDDEN, F32))
        top = jnp.max(top, 0, keepdims=True) * EXP_SCALE
        out_t[:, :n] = jnp.zeros((HD, n), F32)

        def expo_group(g, total):
            ebs = []
            for u in range(GROUP):
                j = g * GROUP + u
                e = jnp.exp2(scores[j, :, :n] * EXP_SCALE - top)
                eb = e.astype(BF16)
                expo[j, :, :n] = eb
                ebs.append(eb)
                total = total + jnp.sum(e.reshape(rows // 8, 8, n), 0)
            keys = pl.ds(pl.multiple_of(g * GROUP * rows, rows), GROUP * rows)
            out_t[:, :n] += jnp.dot(
                value_t[:, keys], jnp.concatenate(ebs, axis=0), preferred_element_type=F32
            )
            return total

        total = lax.fori_loop(0, groups, expo_group, jnp.zeros((8, n), F32))
        inverse = 1.0 / jnp.sum(total, 0, keepdims=True)
        out_b = (out_t[:, :n] * inverse).astype(BF16).astype(F32)
        go = go_t[:, span].astype(F32)
        delta = jnp.sum(go * out_b, 0, keepdims=True) * inverse
        scaled = go * inverse
        gp_t[:, :n] = scaled.astype(BF16)
        for i in range(heads):
            r = off // HD + i
            attn[:, r * HD : (r + 1) * HD] = jnp.transpose(out_b[:, i * rows : (i + 1) * rows]).astype(BF16)
            gp_rows[i * rows : (i + 1) * rows] = jnp.transpose(scaled[:, i * rows : (i + 1) * rows]).astype(BF16)
        return delta

    def give(j, to, when):
        start(remote(pair_send.at[j], pair_recv.at[j], pair_ssem.at[j], pair_rsem.at[j], ctx=to), when)

    def take(j, into, when):
        def add_in():
            arrived(pair_recv.at[j], pair_rsem.at[j])
            pair_acc[into] += pair_recv[j].astype(F32)

        pl.when(when)(add_in)

    def give_sum(j):
        def store():
            pair_send[j] = pair_acc[j].astype(BF16)

        pl.when(c >= j)(store)
        give(j, jnp.maximum(c - j, 0), c >= j)

    def after_group(g):
        for j in reversed(range(g * GROUP, (g + 1) * GROUP)):
            if j % 4:
                give(j, z * 4 + lax.rem(y + 8 - j, 4), c >= j)

    def pair_second():
        for j in (7, 6, 5, 3, 2, 1):
            take(j, 4 * ((y + j) // 4), z * 4 + lax.rem(y + j, 4) >= j)
            if j == 5:
                give_sum(8)
        give_sum(4)

    def pair_third():
        for j in (8, 4):
            take(j, 0, z + j // 4 < rings)

    def backward(s, delta, last):
        off, wide = PIECES[s]
        heads = wide // HD
        n = heads * rows
        first = off // HD * rows
        span = slice(first, first + n)
        dq_t[:, :n] = jnp.zeros((HD, n), F32)

        def group(g):
            all_ds = []
            for u in reversed(range(GROUP)):
                j = g * GROUP + u
                dp = jnp.dot(window[j, rows:seg_at], gp_t[:, :n], preferred_element_type=F32)
                eb = expo[j, :, :n]
                ds = (eb.astype(F32) * (dp - delta)).astype(BF16)
                all_ds.insert(0, ds)
                dk = jnp.dot(ds, q_rows[span], preferred_element_type=F32) * SCALE
                dv = jnp.dot(eb, gp_rows[:n], preferred_element_type=F32)
                if not last:
                    pair_acc[j, :, :HD] = dk
                    pair_acc[j, :, HD:] = dv
                else:
                    dk = dk + pair_acc[j, :, :HD]
                    dv = dv + pair_acc[j, :, HD:]
                    if j % 4 == 0:
                        pair_acc[j, :, :HD] = dk
                        pair_acc[j, :, HD:] = dv
                    else:
                        pair_send[j, :, :HD] = dk.astype(BF16)
                        pair_send[j, :, HD:] = dv.astype(BF16)
            keys = pl.ds(pl.multiple_of(g * GROUP * rows, rows), GROUP * rows)
            dq_t[:, :n] += jnp.dot(
                key_t[:, keys], jnp.concatenate(all_ds, axis=0), preferred_element_type=F32
            )

        if last:
            for g in reversed(range(WINDOW // GROUP + 1)):
                pl.when(g < groups)(functools.partial(group, g))
                after_group(g)
        else:
            pl.loop(0, groups)(group)

        inner = jnp.zeros((1, rows), F32)
        for i in range(heads):
            r = off // HD + i
            one = dq_t[:, i * rows : (i + 1) * rows] * SCALE
            dproj[h, :, r * HD : (r + 1) * HD] = jnp.transpose(one).astype(BF16)
            inner += jnp.sum(one * q_t[:, r * rows : (r + 1) * rows].astype(F32), 0, keepdims=True)
        return inner

    def slot(ref, s, who, lo, size):
        off, wide = PIECES[s]
        return ref.at[who, pl.ds(lo, size), pl.ds(off, wide)]

    def move(s, n, who, lo, size, to):
        start(remote(slot(dproj, s, who, lo, size), slot(dproj, s, who, lo, size),
                     ag_send.at[s, n], ag_recv.at[s, n], head=to))

    def landed_piece(s, n, who, lo, size):
        arrived(slot(dproj, s, who, lo, size), ag_recv.at[s, n])

    def gather_send(s):
        for n, to in enumerate((right, left, far, partner)):
            move(s, n, h, 0, rows, to)

    def gather_pass(s):
        for n, who in enumerate((left, right, far)):
            landed_piece(s, n, who, 0, rows)
            move(s, 4 + n, who, 0, rows, partner)

    def add(s, who, fresh=False):
        off, wide = PIECES[s]
        value = lax.dot_general(
            dproj[who, :, off : off + wide], wv[who, :, off : off + wide],
            (((1,), (1,)), ((), ())), preferred_element_type=F32,
        )
        if fresh:
            dnormed[...] = value
        else:
            dnormed[...] += value

    def add_own(s, fresh=False):
        add(s, h, fresh)
        for who in (left, right, far):
            add(s, who)

    def add_rest(s):
        landed_piece(s, 3, partner, 0, rows)
        add(s, partner)
        for n, d in enumerate((3, 1, 2)):
            who = head_of(x + d, 1 - p)
            landed_piece(s, 4 + n, who, 0, rows)
            add(s, who)

    delta = forward(1)
    inner = backward(1, delta, False)
    gather_send(1)
    queries(2)
    delta = forward(2)
    inner += backward(2, delta, True)
    gather_send(2)
    gather_pass(1)
    add_own(1, True)
    pair_second()
    add_rest(1)
    gather_pass(2)
    pair_third()

    pair_grad = pair_acc[0]
    dproj[h, :, PIECES[0][0] :] = pair_grad.astype(BF16)
    gather_send(0)
    prod = pair_grad[:, :HD] * window[0, :rows].astype(F32) + pair_grad[:, HD:] * window[0, rows:seg_at].astype(F32)
    inner += jnp.sum(jnp.transpose(prod), 0, keepdims=True)
    inner_stats[0] = jnp.broadcast_to(inner, (8, rows))
    small_first(inner_stats, in_send, in_recv)
    add_own(2)
    small_second(inner_stats, in_send, in_recv)
    gather_pass(0)
    add_rest(2)
    add_own(0)
    inner_col = small_total(inner_stats, in_recv)
    add_rest(0)

    scale = recip[:, :1]
    weighted = tok[...].astype(F32) * scale
    gain_part = jnp.sum(dnormed[...] * weighted, 0, keepdims=True)
    lanes = wide_in // 128
    gain_stats[0] = jnp.zeros((8, 128), F32)
    for k in range(lanes):
        gain_stats[0, k : k + 1] = gain_part[:, k * 128 : (k + 1) * 128]
    for d in range(1, n_ctx):
        start(remote(
            gain_stats.at[0], gain_stats.at[d], gg_send.at[d], gg_recv.at[d], ctx=lax.rem(c + d, n_ctx),
        ))
    grad_tokens[...] = (
        dnormed[...] * gain[...].reshape(1, wide_in) * scale - weighted * (scale * inner_col * (1.0 / D))
    ).astype(BF16)
    gain_total = gain_stats[0]
    for d in range(1, n_ctx):
        arrived(gain_stats.at[d], gg_recv.at[d])
        gain_total = gain_total + gain_stats[d]
    grad_gain[...] = gain_total

    for copy, when in started:
        if when is None:
            copy.wait_send()
        else:
            pl.when(when)(copy.wait_send)


def hand_over(attn, grad_tokens, gain_rows, attn_out, grad_out, gain_out):
    attn_out[...] = attn[...]
    grad_out[...] = grad_tokens[...]
    wide = gain_out.shape[0]
    gain_out[...] = gain_rows[: wide // 128].reshape(wide)


def on_device(n_ctx, tokens, gain, qkv_weight, target, advantage, segment):
    rows, wide = tokens.shape
    group = qkv_weight.shape[1] // 8
    n = 3 * rows
    slots = WINDOW + 1
    vmem = pl.BlockSpec(memory_space=pltpu.VMEM)
    anywhere = pl.BlockSpec(memory_space=pl.ANY)
    scratch = [
        ((rows, wide), BF16), ((8, wide, group), BF16),
        ((4, rows, group), BF16), ((4, rows, group), BF16), ((3, rows, group), BF16),
        ((2, rows // 2, group), F32), ((rows, group), F32),
        ((2, rows // 2, group), BF16), ((2, rows, group), BF16), ((rows, 2 * HD), BF16),
        ((6, 8, rows), F32), ((rows, HD), F32), ((slots, 2 * rows + 16, HD), BF16),
        ((HD, slots * rows), BF16), ((HD, slots * rows), BF16), ((slots, rows, rows), F32),
        ((HEADS * rows, HD), BF16), ((HD, HEADS * rows), BF16), ((HD, HEADS * rows), BF16),
        ((slots, rows, n), F32), ((slots, rows, n), BF16), ((HD, n), F32),
        ((n, HD), BF16), ((HD, n), BF16), ((HD, n), F32),
        ((slots, rows, 2 * HD), F32), ((slots, rows, 2 * HD), BF16), ((slots, rows, 2 * HD), BF16),
        ((8, rows, group), BF16), ((6, 8, rows), F32), ((rows, wide), F32), ((n_ctx, 8, 128), F32),
    ]
    sems = [
        (3, 8), (3, 4), (3, 4), (3, 2), (3, 2), (3, 4), (3, 4), (4,), (4,),
        (12,), (slots,), (slots,), (slots,),
        (3, 7), (3, 7), (4,), (4,), (n_ctx,), (n_ctx,),
    ]
    out_types = (
        jax.ShapeDtypeStruct((rows, HEADS * HD), BF16),
        jax.ShapeDtypeStruct((rows, wide), BF16),
    )
    out, grad_tokens, gain_rows = pl.pallas_call(
        functools.partial(kernel, n_ctx),
        out_shape=(*out_types, jax.ShapeDtypeStruct((8, 128), F32)),
        in_specs=[vmem, vmem, anywhere, vmem, vmem, vmem],
        out_specs=(vmem, vmem, vmem),
        scratch_shapes=[pltpu.VMEM(shape, dtype) for shape, dtype in scratch]
        + [pltpu.SemaphoreType.DMA(shape) for shape in sems],
        compiler_params=pltpu.CompilerParams(
            collective_id=0, has_side_effects=True, vmem_limit_bytes=60 * 1024 * 1024
        ),
    )(
        tokens, gain, qkv_weight, target,
        advantage.reshape(1, rows), segment.reshape(1, rows),
    )
    return pl.pallas_call(
        hand_over,
        out_shape=(*out_types, jax.ShapeDtypeStruct((wide,), F32)),
        in_specs=[vmem, vmem, vmem],
        out_specs=(vmem, vmem, vmem),
    )(out, grad_tokens, gain_rows)


def solution(mesh):
    placed = (P("ctx", "head"), P("head"), P("head", None), P("ctx", "head"), P("ctx"), P("ctx"))
    return jax.shard_map(
        functools.partial(on_device, mesh.shape["ctx"]),
        mesh=mesh,
        in_specs=placed,
        out_specs=(P("ctx", "head"), P("ctx", "head"), P("head")),
        check_vma=False,
    )
```

```python
import functools

import jax
import jax.numpy as jnp
from jax import lax
from jax.experimental import pallas as pl
from jax.experimental.pallas import tpu as pltpu
from jax.sharding import PartitionSpec as P

D = 5120
HD = 128
HEADS = 5
WINDOW = 8
EPSILON = 1e-06
SCALE = HD**-0.5
LOG2E = 1.4426950408889634
EXP_SCALE = SCALE * LOG2E
HIDDEN = -1e30
PIECES = ((640, 128), (768, 128), (0, 256), (256, 384))
KEYS, VALUES, FIRST, SECOND = range(4)
GROUP = 3
STEPS = (2, 1, 3, 0)
F32 = jnp.float32
BF16 = jnp.bfloat16


def kernel(
    n_ctx, tok, gain, w_hbm, target, advantage, segment,
    attn, grad_tokens, grad_gain,
    xb, wv, part_send, part_recv, chip_sum, hold, own, relay, landed, landed_far,
    stats, recip, key_win, value_win, key_t, value_t, bias,
    q_rows, q_t, go_t, scores, expo, out_t, gp_rows, gp_t, dq_t, pair_acc, pair_send, pair_recv,
    dproj, inner_stats, dnormed, gain_stats,
    w_sem, ps_send, ps_recv, r1_send, r1_recv, r2_send, r2_recv, st_send, st_recv,
    win_ssem, win_rsem, pair_ssem, pair_rsem,
    ag_send, ag_recv, in_send, in_recv, gg_send, gg_recv,
):
    rows, wide_in = tok.shape
    half = rows // 2
    c = lax.axis_index("ctx")
    h = lax.axis_index("head")
    x = h // 2
    p = lax.rem(h, 2)
    z = c // 4
    y = lax.rem(c, 4)
    rings = n_ctx // 4
    up, down = z * 4 + lax.rem(y + 1, 4), z * 4 + lax.rem(y + 3, 4)

    def head_of(xx, pp):
        return lax.rem(xx + 8, 4) * 2 + pp

    right, left, partner = head_of(x + 1, p), head_of(x - 1, p), head_of(x, 1 - p)
    far = head_of(x + 2, p)
    started = []

    def remote(src, dst, send, recv, **where):
        axis, index = next(iter(where.items()))
        return pltpu.make_async_remote_copy(
            src_ref=src, dst_ref=dst, send_sem=send, recv_sem=recv,
            device_id={axis: index}, device_id_type=pl.DeviceIdType.MESH,
        )

    def start(copy, when=None):
        started.append((copy, when))
        if when is None:
            copy.start()
        else:
            pl.when(when)(copy.start)

    def arrived(dst, recv):
        remote(dst, dst, recv, recv, head=partner).wait_recv()

    barrier = pltpu.get_barrier_semaphore()
    for other in (partner, right, left, head_of(x + 2, p)):
        pl.semaphore_signal(
            barrier, inc=1, device_id={"head": other}, device_id_type=pl.DeviceIdType.MESH
        )
    others = [lax.rem(c + d, n_ctx) for d in range(1, n_ctx)]
    for other in others:
        pl.semaphore_signal(
            barrier, inc=1, device_id={"ctx": other}, device_id_type=pl.DeviceIdType.MESH
        )

    def fetch(s, i):
        off, wide = PIECES[s]
        g = head_of(x + STEPS[i % 4], (1 - p) if i < 4 else p)
        first = pl.multiple_of(g * 896 + off, 128)
        return g, pltpu.make_async_copy(
            w_hbm.at[:, pl.ds(first, wide)], wv.at[g, :, pl.ds(off, wide)], w_sem.at[s, i]
        )

    for s in range(4):
        for i in range(8):
            fetch(s, i)[1].start()

    gain_row = gain[...].reshape(1, wide_in)
    xb[...] = (tok[...].astype(F32) * gain_row).astype(BF16)

    def project(s):
        off, wide = PIECES[s]
        cols = pl.ds(off, wide)
        for i in range(4):
            g, copy = fetch(s, i)
            copy.wait()
            part_send[i, :, off : off + wide] = jnp.dot(
                xb[...], wv[g, :, off : off + wide], preferred_element_type=F32
            ).astype(BF16)
            if s == 0 and i == 0:
                pl.semaphore_wait(barrier, 4 + len(others))
            start(remote(
                part_send.at[i, :, cols], part_recv.at[i, :, cols],
                ps_send.at[s, i], ps_recv.at[s, i], head=partner,
            ))
        for i in range(4):
            g, copy = fetch(s, 4 + i)
            copy.wait()
            mine = jnp.dot(xb[...], wv[g, :, off : off + wide], preferred_element_type=F32)
            arrived(part_recv.at[i, :, cols], ps_recv.at[s, i])
            mine = mine + part_recv[i, :, off : off + wide].astype(F32)
            if i < 3:
                chip_sum[i, :, off : off + wide] = mine.astype(BF16)
            top = pl.ds(0, half)
            low = pl.ds(half, half)
            if s < 2 and i < 3:
                start(remote(
                    chip_sum.at[i, :, cols], (landed_far.at[s], landed.at[0, :, cols], landed.at[1, :, cols])[i],
                    r2_send.at[s, i], r2_recv.at[s, i], head=(far, right, left)[i],
                ))
            elif i == 0:
                start(remote(
                    chip_sum.at[0, top, cols], relay.at[0, :, cols],
                    r1_send.at[s, 0], r1_recv.at[s, 0], head=right,
                ))
                start(remote(
                    chip_sum.at[0, low, cols], relay.at[1, :, cols],
                    r1_send.at[s, 1], r1_recv.at[s, 1], head=left,
                ))
            elif i == 1:
                hold[0, :, off : off + wide] = mine[:half]
                start(remote(
                    chip_sum.at[1, low, cols], landed.at[0, low, cols],
                    r2_send.at[s, 0], r2_recv.at[s, 0], head=right,
                ))
            elif i == 2:
                hold[1, :, off : off + wide] = mine[half:]
                start(remote(
                    chip_sum.at[2, top, cols], landed.at[1, top, cols],
                    r2_send.at[s, 1], r2_recv.at[s, 1], head=left,
                ))
            else:
                own[:, off : off + wide] = mine

    def pass_on(s):
        off, wide = PIECES[s]
        cols = pl.ds(off, wide)
        top = pl.ds(0, half)
        low = pl.ds(half, half)
        arrived(relay.at[0, :, cols], r1_recv.at[s, 0])
        chip_sum[1, :half, off : off + wide] = (
            hold[0, :, off : off + wide] + relay[0, :, off : off + wide].astype(F32)
        ).astype(BF16)
        start(remote(
            chip_sum.at[1, top, cols], landed.at[0, top, cols],
            r2_send.at[s, 2], r2_recv.at[s, 2], head=right,
        ))
        arrived(relay.at[1, :, cols], r1_recv.at[s, 1])
        chip_sum[2, half:, off : off + wide] = (
            hold[1, :, off : off + wide] + relay[1, :, off : off + wide].astype(F32)
        ).astype(BF16)
        start(remote(
            chip_sum.at[2, low, cols], landed.at[1, low, cols],
            r2_send.at[s, 3], r2_recv.at[s, 3], head=left,
        ))

    def finish(s):
        off, wide = PIECES[s]
        cols = pl.ds(off, wide)
        top = pl.ds(0, half)
        low = pl.ds(half, half)
        if s < 2:
            arrived(landed_far.at[s], r2_recv.at[s, 0])
            arrived(landed.at[0, :, cols], r2_recv.at[s, 1])
            arrived(landed.at[1, :, cols], r2_recv.at[s, 2])
        else:
            arrived(landed.at[0, low, cols], r2_recv.at[s, 0])
            arrived(landed.at[1, top, cols], r2_recv.at[s, 1])
            arrived(landed.at[0, top, cols], r2_recv.at[s, 2])
            arrived(landed.at[1, low, cols], r2_recv.at[s, 3])
        total = own[:, off : off + wide] + landed[0, :, off : off + wide].astype(F32)
        total = total + landed[1, :, off : off + wide].astype(F32)
        if s < 2:
            total = total + landed_far[s].astype(F32)
        scale = recip[:, :1]
        return (total * scale).astype(BF16)

    def small_first(ref, send, recv):
        start(remote(ref.at[0], ref.at[1], send.at[0], recv.at[0], head=partner))

    def small_second(ref, send, recv):
        arrived(ref.at[1], recv.at[0])
        ref[2] = ref[0] + ref[1]
        for d in range(1, 4):
            start(remote(ref.at[2], ref.at[2 + d], send.at[d], recv.at[d], head=head_of(x + d, p)))

    def small_total(ref, recv):
        for d in range(1, 4):
            arrived(ref.at[2 + d], recv.at[d])
        return jnp.transpose(ref[2] + ref[3] + ref[4] + ref[5])[:, :1]

    project(KEYS)
    features = tok[...].astype(F32)
    stats[0] = lax.dot_general(
        jnp.ones((8, wide_in), F32), features * features, (((1,), (1,)), ((), ())),
        precision=lax.Precision.HIGHEST, preferred_element_type=F32,
    )
    small_first(stats, st_send, st_recv)
    project(VALUES)
    small_second(stats, st_send, st_recv)
    seg_row = segment[...].astype(F32)
    which = lax.broadcasted_iota(jnp.int32, (16, HD), 0)
    seg_block = jnp.zeros((16, HD), F32)
    for k in range(rows // HD):
        seg_block = jnp.where(which == k, seg_row[:, k * HD : (k + 1) * HD], seg_block)
    key_win[0, rows:] = seg_block.astype(BF16)
    project(FIRST)
    recip[...] = jnp.broadcast_to(
        lax.rsqrt(small_total(stats, st_recv) / D + EPSILON), (rows, HD)
    )

    windows = (key_win, value_win)

    def share(w, n, src, dst, to, when):
        start(remote(
            windows[w].at[src], windows[w].at[dst], win_ssem.at[w, n], win_rsem.at[w, dst], ctx=to,
        ), when)

    def here(w, j):
        pl.when(c >= j)(lambda: arrived(windows[w].at[j], win_rsem.at[w, j]))

    def share_first(w):
        for d in (1, 2):
            share(w, d, 0, 4 * d, jnp.minimum(c + 4 * d, n_ctx - 1), z + d < rings)
        for d in range(1, 4):
            share(w, 2 + d, 0, d, z * 4 + jnp.minimum(y + d, 3), y + d <= 3)

    def share_second(w):
        here(w, 4)
        for d in (1, 3, 2):
            share(w, 5 + d, 4, 4 + d - 4 * ((y + d) // 4), z * 4 + lax.rem(y + d, 4), z >= 1)

    def share_third(w):
        here(w, 8)
        for d in range(1, 4):
            share(w, 8 + d, 8, 8 - d, z * 4 + jnp.maximum(y - d, 0), (z >= 2) & (y >= d))

    def share_last(w):
        for j in (1, 2, 3, 5, 6, 7):
            here(w, j)

    key_win[0, :rows] = finish(KEYS)
    share_first(0)
    project(SECOND)
    value_win[0] = finish(VALUES)
    share_first(1)
    pass_on(FIRST)
    share_second(0)
    share_third(0)
    share_second(1)
    share_third(1)
    pass_on(SECOND)

    factor = 0.25 * advantage[...].astype(F32)
    for r in range(HEADS):
        block = jnp.transpose(target[:, r * HD : (r + 1) * HD].astype(F32))
        go_t[:, r * rows : (r + 1) * rows] = (block * factor).astype(BF16)

    def queries(s):
        q = finish(s)
        first = PIECES[s][0] // HD
        for i in range(PIECES[s][1] // HD):
            one = q[:, i * HD : (i + 1) * HD]
            q_rows[(first + i) * rows : (first + i + 1) * rows] = one
            q_t[:, (first + i) * rows : (first + i + 1) * rows] = jnp.transpose(one.astype(F32)).astype(BF16)

    queries(FIRST)
    share_last(0)

    blocks = jnp.minimum(c, WINDOW) + 1
    groups = (blocks + GROUP - 1) // GROUP

    def prepare_keys(j, diagonal):
        key_t[:, pl.ds(pl.multiple_of(j * rows, rows), rows)] = (
            jnp.transpose(key_win[j, :rows].astype(F32)).astype(BF16)
        )
        ids = jnp.transpose(key_win[j, rows:].astype(F32))
        for k in range(rows // HD):
            visible = ids[:, k : k + 1] == seg_row
            if diagonal:
                k_pos = lax.broadcasted_iota(jnp.int32, (HD, rows), 0) + k * HD
                q_pos = lax.broadcasted_iota(jnp.int32, (HD, rows), 1)
                visible = visible & (k_pos <= q_pos)
            bias[j, k * HD : (k + 1) * HD] = jnp.where(visible, 0.0, HIDDEN)

    prepare_keys(0, True)

    @pl.loop(1, blocks)
    def _(j):
        prepare_keys(j, False)

    @pl.loop(blocks, groups * GROUP)
    def _(j):
        span = pl.ds(pl.multiple_of(j * rows, rows), rows)
        key_win[j] = jnp.zeros((rows + 16, HD), BF16)
        value_win[j] = jnp.zeros((rows, HD), BF16)
        key_t[:, span] = jnp.zeros((HD, rows), BF16)
        bias[j] = jnp.full((rows, rows), HIDDEN, F32)

    def prepare_values():
        @pl.loop(0, groups * GROUP)
        def _(j):
            value_t[:, pl.ds(pl.multiple_of(j * rows, rows), rows)] = (
                jnp.transpose(value_win[j].astype(F32)).astype(BF16)
            )

    def part(s):
        off, wide = PIECES[s]
        heads = wide // HD
        return off // HD, heads, pl.ds(off // HD * rows, heads * rows), heads * rows

    def score(s):
        _, heads, span, n = part(s)

        def score_group(g, top):
            for u in range(GROUP):
                j = g * GROUP + u
                block = jnp.dot(key_win[j, :rows], q_t[:, span], preferred_element_type=F32)
                block = block + jnp.concatenate([bias[j]] * heads, axis=1)
                scores[j, :, span] = block
                top = jnp.maximum(top, jnp.max(block.reshape(rows // 8, 8, n), 0))
            return top

        top = lax.fori_loop(0, groups, score_group, jnp.full((8, n), HIDDEN, F32))
        return jnp.max(top, 0, keepdims=True) * EXP_SCALE

    def output(s, top):
        first, heads, span, n = part(s)
        out_t[:, :n] = jnp.zeros((HD, n), F32)

        def expo_group(g, total):
            ebs = []
            for u in range(GROUP):
                j = g * GROUP + u
                e = jnp.exp2(scores[j, :, span] * EXP_SCALE - top)
                eb = e.astype(BF16)
                expo[j, :, span] = eb
                ebs.append(eb)
                total = total + jnp.sum(e.reshape(rows // 8, 8, n), 0)
            keys = pl.ds(pl.multiple_of(g * GROUP * rows, rows), GROUP * rows)
            out_t[:, :n] += jnp.dot(
                value_t[:, keys], jnp.concatenate(ebs, axis=0), preferred_element_type=F32
            )
            return total

        total = lax.fori_loop(0, groups, expo_group, jnp.zeros((8, n), F32))
        inverse = 1.0 / jnp.sum(total, 0, keepdims=True)
        out_b = (out_t[:, :n] * inverse).astype(BF16).astype(F32)
        go = go_t[:, span].astype(F32)
        delta = jnp.sum(go * out_b, 0, keepdims=True) * inverse
        scaled = go * inverse
        gp_t[:, span] = scaled.astype(BF16)
        for i in range(heads):
            r = first + i
            attn[:, r * HD : (r + 1) * HD] = jnp.transpose(out_b[:, i * rows : (i + 1) * rows]).astype(BF16)
            gp_rows[r * rows : (r + 1) * rows] = jnp.transpose(scaled[:, i * rows : (i + 1) * rows]).astype(BF16)
        return delta

    def give(w, j, to, when):
        start(remote(
            pair_send.at[w, j], pair_recv.at[w, j], pair_ssem.at[w, j], pair_rsem.at[w, j], ctx=to,
        ), when)

    def take(w, j, into, when):
        def add_in():
            arrived(pair_recv.at[w, j], pair_rsem.at[w, j])
            pair_acc[w, into] += pair_recv[w, j].astype(F32)

        pl.when(when)(add_in)

    def give_sum(w, j):
        def store():
            pair_send[w, j] = pair_acc[w, j].astype(BF16)

        pl.when(c >= j)(store)
        give(w, j, jnp.maximum(c - j, 0), c >= j)

    def keep(w, j, value):
        if j % 4 == 0:
            pair_acc[w, j // 4 * 4] = value
        else:
            pair_send[w, j] = value.astype(BF16)

    def after_group(w, g):
        for j in reversed(range(g * GROUP, (g + 1) * GROUP)):
            if j % 4:
                give(w, j, z * 4 + lax.rem(y + 8 - j, 4), c >= j)

    def pair_second(w):
        for j in (7, 6, 5, 3, 2, 1):
            take(w, j, 4 * ((y + j) // 4), z * 4 + lax.rem(y + j, 4) >= j)
            if j == 5:
                give_sum(w, 8)
        give_sum(w, 4)

    def pair_third(w):
        for j in (8, 4):
            take(w, j, 0, z + j // 4 < rings)

    def backward_values():
        def group(g):
            for u in reversed(range(GROUP)):
                j = g * GROUP + u
                keep(1, j, jnp.dot(expo[j], gp_rows[...], preferred_element_type=F32))

        for g in reversed(range(WINDOW // GROUP + 1)):
            pl.when(g < groups)(functools.partial(group, g))
            after_group(1, g)

    def score_gradients(s, j, delta):
        _, _, span, _ = part(s)
        dp = jnp.dot(value_win[j], gp_t[:, span], preferred_element_type=F32)
        expo[j, :, span] = (expo[j, :, span].astype(F32) * (dp - delta)).astype(BF16)

    def backward_first(delta):
        @pl.loop(0, groups)
        def _(g):
            for u in range(GROUP):
                score_gradients(FIRST, g * GROUP + u, delta)

    def backward_keys(delta):
        def group(g):
            for u in reversed(range(GROUP)):
                j = g * GROUP + u
                score_gradients(SECOND, j, delta)
                keep(0, j, jnp.dot(expo[j], q_rows[...], preferred_element_type=F32) * SCALE)

        for g in reversed(range(WINDOW // GROUP + 1)):
            pl.when(g < groups)(functools.partial(group, g))
            after_group(0, g)

    def backward_queries(s):
        first, heads, span, n = part(s)
        dq_t[:, :n] = jnp.zeros((HD, n), F32)

        @pl.loop(0, groups)
        def _(g):
            keys = pl.ds(pl.multiple_of(g * GROUP * rows, rows), GROUP * rows)
            ds = jnp.concatenate([expo[g * GROUP + u, :, span] for u in range(GROUP)], axis=0)
            dq_t[:, :n] += jnp.dot(key_t[:, keys], ds, preferred_element_type=F32)

        inner = jnp.zeros((1, rows), F32)
        for i in range(heads):
            r = first + i
            one = dq_t[:, i * rows : (i + 1) * rows] * SCALE
            dproj[h, :, r * HD : (r + 1) * HD] = jnp.transpose(one).astype(BF16)
            inner += jnp.sum(one * q_t[:, r * rows : (r + 1) * rows].astype(F32), 0, keepdims=True)
        return inner

    def slot(ref, s, who, lo, size):
        off, wide = PIECES[s]
        return ref.at[who, pl.ds(lo, size), pl.ds(off, wide)]

    def move(s, n, who, lo, size, to):
        start(remote(slot(dproj, s, who, lo, size), slot(dproj, s, who, lo, size),
                     ag_send.at[s, n], ag_recv.at[s, n], head=to))

    def landed_piece(s, n, who, lo, size):
        arrived(slot(dproj, s, who, lo, size), ag_recv.at[s, n])

    def gather_send(s):
        for n, to in enumerate((right, left, far, partner)):
            move(s, n, h, 0, rows, to)

    def gather_pass(s):
        for n, who in enumerate((left, right, far)):
            landed_piece(s, n, who, 0, rows)
            move(s, 4 + n, who, 0, rows, partner)

    def add(s, who, fresh=False):
        off, wide = PIECES[s]
        value = lax.dot_general(
            dproj[who, :, off : off + wide], wv[who, :, off : off + wide],
            (((1,), (1,)), ((), ())), preferred_element_type=F32,
        )
        if fresh:
            dnormed[...] = value
        else:
            dnormed[...] += value

    def add_own(s, fresh=False):
        add(s, h, fresh)
        for who in (left, right, far):
            add(s, who)

    def add_rest(s):
        landed_piece(s, 3, partner, 0, rows)
        add(s, partner)
        for n, d in enumerate((3, 1, 2)):
            who = head_of(x + d, 1 - p)
            landed_piece(s, 4 + n, who, 0, rows)
            add(s, who)

    top = score(FIRST)
    share_last(1)
    prepare_values()
    delta_first = output(FIRST, top)
    queries(SECOND)
    delta_second = output(SECOND, score(SECOND))
    backward_values()
    backward_first(delta_first)
    inner = backward_queries(FIRST)
    gather_send(FIRST)
    backward_keys(delta_second)
    inner += backward_queries(SECOND)
    gather_send(SECOND)
    pair_second(1)
    gather_pass(FIRST)
    add_own(FIRST, True)
    pair_second(0)
    pair_third(1)
    dproj[h, :, PIECES[VALUES][0] :] = pair_acc[1, 0].astype(BF16)
    gather_send(VALUES)
    add_rest(FIRST)
    gather_pass(SECOND)
    pair_third(0)
    dproj[h, :, PIECES[KEYS][0] : PIECES[VALUES][0]] = pair_acc[0, 0].astype(BF16)
    gather_send(KEYS)
    prod = pair_acc[0, 0] * key_win[0, :rows].astype(F32) + pair_acc[1, 0] * value_win[0].astype(F32)
    inner += jnp.sum(jnp.transpose(prod), 0, keepdims=True)
    inner_stats[0] = jnp.broadcast_to(inner, (8, rows))
    small_first(inner_stats, in_send, in_recv)
    add_own(SECOND)
    add_rest(SECOND)
    gather_pass(VALUES)
    small_second(inner_stats, in_send, in_recv)
    add_own(VALUES)
    add_rest(VALUES)
    gather_pass(KEYS)
    add_own(KEYS)
    inner_col = small_total(inner_stats, in_recv)
    add_rest(KEYS)

    scale = recip[:, :1]
    weighted = tok[...].astype(F32) * scale
    gain_part = jnp.sum(dnormed[...] * weighted, 0, keepdims=True)
    lanes = wide_in // 128
    gain_stats[0] = jnp.zeros((8, 128), F32)
    for k in range(lanes):
        gain_stats[0, k : k + 1] = gain_part[:, k * 128 : (k + 1) * 128]
    for d in range(1, n_ctx):
        start(remote(
            gain_stats.at[0], gain_stats.at[d], gg_send.at[d], gg_recv.at[d], ctx=lax.rem(c + d, n_ctx),
        ))
    grad_tokens[...] = (
        dnormed[...] * gain[...].reshape(1, wide_in) * scale - weighted * (scale * inner_col * (1.0 / D))
    ).astype(BF16)
    gain_total = gain_stats[0]
    for d in range(1, n_ctx):
        arrived(gain_stats.at[d], gg_recv.at[d])
        gain_total = gain_total + gain_stats[d]
    grad_gain[...] = gain_total

    for copy, when in started:
        if when is None:
            copy.wait_send()
        else:
            pl.when(when)(copy.wait_send)


def hand_over(attn, grad_tokens, gain_rows, attn_out, grad_out, gain_out):
    attn_out[...] = attn[...]
    grad_out[...] = grad_tokens[...]
    wide = gain_out.shape[0]
    gain_out[...] = gain_rows[: wide // 128].reshape(wide)


def on_device(n_ctx, tokens, gain, qkv_weight, target, advantage, segment):
    rows, wide = tokens.shape
    group = qkv_weight.shape[1] // 8
    n = 3 * rows
    every = HEADS * rows
    slots = WINDOW + 1
    vmem = pl.BlockSpec(memory_space=pltpu.VMEM)
    anywhere = pl.BlockSpec(memory_space=pl.ANY)
    scratch = [
        ((rows, wide), BF16), ((8, wide, group), BF16),
        ((4, rows, group), BF16), ((4, rows, group), BF16), ((3, rows, group), BF16),
        ((2, rows // 2, group), F32), ((rows, group), F32),
        ((2, rows // 2, group), BF16), ((2, rows, group), BF16), ((2, rows, HD), BF16),
        ((6, 8, rows), F32), ((rows, HD), F32),
        ((slots, rows + 16, HD), BF16), ((slots, rows, HD), BF16),
        ((HD, slots * rows), BF16), ((HD, slots * rows), BF16), ((slots, rows, rows), F32),
        ((HEADS * rows, HD), BF16), ((HD, HEADS * rows), BF16), ((HD, HEADS * rows), BF16),
        ((slots, rows, every), F32), ((slots, rows, every), BF16), ((HD, n), F32),
        ((every, HD), BF16), ((HD, every), BF16), ((HD, n), F32),
        ((2, slots, rows, HD), F32), ((2, slots, rows, HD), BF16), ((2, slots, rows, HD), BF16),
        ((8, rows, group), BF16), ((6, 8, rows), F32), ((rows, wide), F32), ((n_ctx, 8, 128), F32),
    ]
    sems = [
        (4, 8), (4, 4), (4, 4), (4, 2), (4, 2), (4, 4), (4, 4), (4,), (4,),
        (2, 12), (2, slots), (2, slots), (2, slots),
        (4, 7), (4, 7), (4,), (4,), (n_ctx,), (n_ctx,),
    ]
    out_types = (
        jax.ShapeDtypeStruct((rows, HEADS * HD), BF16),
        jax.ShapeDtypeStruct((rows, wide), BF16),
    )
    out, grad_tokens, gain_rows = pl.pallas_call(
        functools.partial(kernel, n_ctx),
        out_shape=(*out_types, jax.ShapeDtypeStruct((8, 128), F32)),
        in_specs=[vmem, vmem, anywhere, vmem, vmem, vmem],
        out_specs=(vmem, vmem, vmem),
        scratch_shapes=[pltpu.VMEM(shape, dtype) for shape, dtype in scratch]
        + [pltpu.SemaphoreType.DMA(shape) for shape in sems],
        compiler_params=pltpu.CompilerParams(
            collective_id=0, has_side_effects=True, vmem_limit_bytes=60 * 1024 * 1024
        ),
    )(
        tokens, gain, qkv_weight, target,
        advantage.reshape(1, rows), segment.reshape(1, rows),
    )
    return pl.pallas_call(
        hand_over,
        out_shape=(*out_types, jax.ShapeDtypeStruct((wide,), F32)),
        in_specs=[vmem, vmem, vmem],
        out_specs=(vmem, vmem, vmem),
    )(out, grad_tokens, gain_rows)


def solution(mesh):
    placed = (P("ctx", "head"), P("head"), P("head", None), P("ctx", "head"), P("ctx"), P("ctx"))
    return jax.shard_map(
        functools.partial(on_device, mesh.shape["ctx"]),
        mesh=mesh,
        in_specs=placed,
        out_specs=(P("ctx", "head"), P("ctx", "head"), P("head")),
        check_vma=False,
    )
```

```python
import functools

import jax
import jax.numpy as jnp
from jax import lax
from jax.experimental import pallas as pl
from jax.experimental.pallas import tpu as pltpu
from jax.sharding import PartitionSpec as P

D = 5120
HD = 128
HEADS = 5
WINDOW = 8
EPSILON = 1e-06
SCALE = HD**-0.5
LOG2E = 1.4426950408889634
EXP_SCALE = SCALE * LOG2E
HIDDEN = -1e30
PIECES = ((640, 128), (768, 128), (0, 256), (256, 384))
KEYS, VALUES, FIRST, SECOND = range(4)
GROUP = 3
STEPS = (2, 1, 3, 0)
F32 = jnp.float32
BF16 = jnp.bfloat16


def kernel(
    n_ctx, tok, gain, w_hbm, target, advantage, segment,
    attn, grad_tokens, grad_gain,
    xb, wv, part_send, part_recv, chip_sum, hold, own, relay, landed, landed_far,
    stats, recip, key_win, value_win, key_t, value_t, bias,
    q_rows, q_t, go_t, scores, expo, out_t, gp_rows, gp_t, dq_t, pair_acc, pair_send, pair_recv,
    dproj, inner_stats, dnormed, gain_stats,
    w_sem, ps_send, ps_recv, r1_send, r1_recv, r2_send, r2_recv, st_send, st_recv,
    win_ssem, win_rsem, pair_ssem, pair_rsem,
    ag_send, ag_recv, in_send, in_recv, gg_send, gg_recv,
):
    rows, wide_in = tok.shape
    half = rows // 2
    c = lax.axis_index("ctx")
    h = lax.axis_index("head")
    x = h // 2
    p = lax.rem(h, 2)
    z = c // 4
    y = lax.rem(c, 4)
    rings = n_ctx // 4
    up, down = z * 4 + lax.rem(y + 1, 4), z * 4 + lax.rem(y + 3, 4)

    def head_of(xx, pp):
        return lax.rem(xx + 8, 4) * 2 + pp

    right, left, partner = head_of(x + 1, p), head_of(x - 1, p), head_of(x, 1 - p)
    far = head_of(x + 2, p)
    started = []

    def remote(src, dst, send, recv, **where):
        axis, index = next(iter(where.items()))
        return pltpu.make_async_remote_copy(
            src_ref=src, dst_ref=dst, send_sem=send, recv_sem=recv,
            device_id={axis: index}, device_id_type=pl.DeviceIdType.MESH,
        )

    def start(copy, when=None):
        started.append((copy, when))
        if when is None:
            copy.start()
        else:
            pl.when(when)(copy.start)

    def arrived(dst, recv):
        remote(dst, dst, recv, recv, head=partner).wait_recv()

    barrier = pltpu.get_barrier_semaphore()
    for other in (partner, right, left, head_of(x + 2, p)):
        pl.semaphore_signal(
            barrier, inc=1, device_id={"head": other}, device_id_type=pl.DeviceIdType.MESH
        )
    others = [lax.rem(c + d, n_ctx) for d in range(1, n_ctx)]
    for other in others:
        pl.semaphore_signal(
            barrier, inc=1, device_id={"ctx": other}, device_id_type=pl.DeviceIdType.MESH
        )

    def fetch(s, i):
        off, wide = PIECES[s]
        g = head_of(x + STEPS[i % 4], (1 - p) if i < 4 else p)
        first = pl.multiple_of(g * 896 + off, 128)
        return g, pltpu.make_async_copy(
            w_hbm.at[:, pl.ds(first, wide)], wv.at[g, :, pl.ds(off, wide)], w_sem.at[s, i]
        )

    for s in range(4):
        for i in range(8):
            fetch(s, i)[1].start()

    gain_row = gain[...].reshape(1, wide_in)
    features = tok[...].astype(F32)
    xb[...] = (features * gain_row).astype(BF16)
    squares = jnp.sum(features * features, -1, keepdims=True)
    stats[0] = jnp.transpose(jnp.broadcast_to(squares, (rows, HD)))[:8]

    def project(s):
        off, wide = PIECES[s]
        cols = pl.ds(off, wide)
        for i in range(4):
            g, copy = fetch(s, i)
            copy.wait()
            part_send[i, :, off : off + wide] = jnp.dot(
                xb[...], wv[g, :, off : off + wide], preferred_element_type=F32
            ).astype(BF16)
            if s == 0 and i == 0:
                pl.semaphore_wait(barrier, 4 + len(others))
                small_first(stats, st_send, st_recv)
            start(remote(
                part_send.at[i, :, cols], part_recv.at[i, :, cols],
                ps_send.at[s, i], ps_recv.at[s, i], head=partner,
            ))
        if s == KEYS:
            small_second(stats, st_send, st_recv)
        for i in range(4):
            g, copy = fetch(s, 4 + i)
            copy.wait()
            mine = jnp.dot(xb[...], wv[g, :, off : off + wide], preferred_element_type=F32)
            arrived(part_recv.at[i, :, cols], ps_recv.at[s, i])
            mine = mine + part_recv[i, :, off : off + wide].astype(F32)
            if i < 3:
                chip_sum[i, :, off : off + wide] = mine.astype(BF16)
            top = pl.ds(0, half)
            low = pl.ds(half, half)
            if s < 2 and i < 3:
                start(remote(
                    chip_sum.at[i, :, cols], (landed_far.at[s], landed.at[0, :, cols], landed.at[1, :, cols])[i],
                    r2_send.at[s, i], r2_recv.at[s, i], head=(far, right, left)[i],
                ))
            elif i == 0:
                start(remote(
                    chip_sum.at[0, top, cols], relay.at[0, :, cols],
                    r1_send.at[s, 0], r1_recv.at[s, 0], head=right,
                ))
                start(remote(
                    chip_sum.at[0, low, cols], relay.at[1, :, cols],
                    r1_send.at[s, 1], r1_recv.at[s, 1], head=left,
                ))
            elif i == 1:
                hold[0, :, off : off + wide] = mine[:half]
                start(remote(
                    chip_sum.at[1, low, cols], landed.at[0, low, cols],
                    r2_send.at[s, 0], r2_recv.at[s, 0], head=right,
                ))
            elif i == 2:
                hold[1, :, off : off + wide] = mine[half:]
                start(remote(
                    chip_sum.at[2, top, cols], landed.at[1, top, cols],
                    r2_send.at[s, 1], r2_recv.at[s, 1], head=left,
                ))
            else:
                own[:, off : off + wide] = mine

    def pass_on(s):
        off, wide = PIECES[s]
        cols = pl.ds(off, wide)
        top = pl.ds(0, half)
        low = pl.ds(half, half)
        arrived(relay.at[0, :, cols], r1_recv.at[s, 0])
        chip_sum[1, :half, off : off + wide] = (
            hold[0, :, off : off + wide] + relay[0, :, off : off + wide].astype(F32)
        ).astype(BF16)
        start(remote(
            chip_sum.at[1, top, cols], landed.at[0, top, cols],
            r2_send.at[s, 2], r2_recv.at[s, 2], head=right,
        ))
        arrived(relay.at[1, :, cols], r1_recv.at[s, 1])
        chip_sum[2, half:, off : off + wide] = (
            hold[1, :, off : off + wide] + relay[1, :, off : off + wide].astype(F32)
        ).astype(BF16)
        start(remote(
            chip_sum.at[2, low, cols], landed.at[1, low, cols],
            r2_send.at[s, 3], r2_recv.at[s, 3], head=left,
        ))

    def finish(s):
        off, wide = PIECES[s]
        cols = pl.ds(off, wide)
        top = pl.ds(0, half)
        low = pl.ds(half, half)
        if s < 2:
            arrived(landed_far.at[s], r2_recv.at[s, 0])
            arrived(landed.at[0, :, cols], r2_recv.at[s, 1])
            arrived(landed.at[1, :, cols], r2_recv.at[s, 2])
        else:
            arrived(landed.at[0, low, cols], r2_recv.at[s, 0])
            arrived(landed.at[1, top, cols], r2_recv.at[s, 1])
            arrived(landed.at[0, top, cols], r2_recv.at[s, 2])
            arrived(landed.at[1, low, cols], r2_recv.at[s, 3])
        total = own[:, off : off + wide] + landed[0, :, off : off + wide].astype(F32)
        total = total + landed[1, :, off : off + wide].astype(F32)
        if s < 2:
            total = total + landed_far[s].astype(F32)
        scale = recip[:, :1]
        return (total * scale).astype(BF16)

    def small_first(ref, send, recv):
        start(remote(ref.at[0], ref.at[1], send.at[0], recv.at[0], head=partner))

    def small_second(ref, send, recv):
        arrived(ref.at[1], recv.at[0])
        ref[2] = ref[0] + ref[1]
        for d in range(1, 4):
            start(remote(ref.at[2], ref.at[2 + d], send.at[d], recv.at[d], head=head_of(x + d, p)))

    def small_total(ref, recv):
        for d in range(1, 4):
            arrived(ref.at[2 + d], recv.at[d])
        return jnp.transpose(ref[2] + ref[3] + ref[4] + ref[5])[:, :1]

    project(KEYS)
    project(VALUES)
    seg_row = segment[...].astype(F32)
    which = lax.broadcasted_iota(jnp.int32, (16, HD), 0)
    seg_block = jnp.zeros((16, HD), F32)
    for k in range(rows // HD):
        seg_block = jnp.where(which == k, seg_row[:, k * HD : (k + 1) * HD], seg_block)
    key_win[0, rows:] = seg_block.astype(BF16)
    project(FIRST)
    recip[...] = jnp.broadcast_to(
        lax.rsqrt(small_total(stats, st_recv) / D + EPSILON), (rows, HD)
    )

    windows = (key_win, value_win)

    def share(w, n, src, dst, to, when):
        start(remote(
            windows[w].at[src], windows[w].at[dst], win_ssem.at[w, n], win_rsem.at[w, dst], ctx=to,
        ), when)

    def here(w, j):
        pl.when(c >= j)(lambda: arrived(windows[w].at[j], win_rsem.at[w, j]))

    def share_first(w):
        for d in (1, 2):
            share(w, d, 0, 4 * d, jnp.minimum(c + 4 * d, n_ctx - 1), z + d < rings)
        for d in range(1, 4):
            share(w, 2 + d, 0, d, z * 4 + jnp.minimum(y + d, 3), y + d <= 3)

    def share_second(w):
        here(w, 4)
        for d in (1, 3, 2):
            share(w, 5 + d, 4, 4 + d - 4 * ((y + d) // 4), z * 4 + lax.rem(y + d, 4), z >= 1)

    def share_third(w):
        here(w, 8)
        for d in range(1, 4):
            share(w, 8 + d, 8, 8 - d, z * 4 + jnp.maximum(y - d, 0), (z >= 2) & (y >= d))

    def share_last(w):
        for j in (1, 2, 3, 5, 6, 7):
            here(w, j)

    key_win[0, :rows] = finish(KEYS)
    share_first(0)
    project(SECOND)
    value_win[0] = finish(VALUES)
    share_first(1)
    pass_on(FIRST)
    share_second(0)
    share_third(0)
    share_second(1)
    share_third(1)
    pass_on(SECOND)

    factor = 0.25 * advantage[...].astype(F32)
    for r in range(HEADS):
        block = jnp.transpose(target[:, r * HD : (r + 1) * HD].astype(F32))
        go_t[:, r * rows : (r + 1) * rows] = (block * factor).astype(BF16)

    def queries(s):
        q = finish(s)
        first = PIECES[s][0] // HD
        for i in range(PIECES[s][1] // HD):
            one = q[:, i * HD : (i + 1) * HD]
            q_rows[(first + i) * rows : (first + i + 1) * rows] = one
            q_t[:, (first + i) * rows : (first + i + 1) * rows] = jnp.transpose(one.astype(F32)).astype(BF16)

    queries(FIRST)
    share_last(0)

    blocks = jnp.minimum(c, WINDOW) + 1
    groups = (blocks + GROUP - 1) // GROUP

    def prepare_keys(j, diagonal):
        key_t[:, pl.ds(pl.multiple_of(j * rows, rows), rows)] = (
            jnp.transpose(key_win[j, :rows].astype(F32)).astype(BF16)
        )
        ids = jnp.transpose(key_win[j, rows:].astype(F32))
        for k in range(rows // HD):
            visible = ids[:, k : k + 1] == seg_row
            if diagonal:
                k_pos = lax.broadcasted_iota(jnp.int32, (HD, rows), 0) + k * HD
                q_pos = lax.broadcasted_iota(jnp.int32, (HD, rows), 1)
                visible = visible & (k_pos <= q_pos)
            bias[j, k * HD : (k + 1) * HD] = jnp.where(visible, 0.0, HIDDEN)

    prepare_keys(0, True)

    @pl.loop(1, blocks)
    def _(j):
        prepare_keys(j, False)

    @pl.loop(blocks, groups * GROUP)
    def _(j):
        span = pl.ds(pl.multiple_of(j * rows, rows), rows)
        key_win[j] = jnp.zeros((rows + 16, HD), BF16)
        value_win[j] = jnp.zeros((rows, HD), BF16)
        key_t[:, span] = jnp.zeros((HD, rows), BF16)
        value_t[:, span] = jnp.zeros((HD, rows), BF16)
        bias[j] = jnp.full((rows, rows), HIDDEN, F32)

    def prepare_values():
        for j in (0, 4, 1, 2, 3, 8, 5, 6, 7):
            if j % 4:
                here(1, j)

            def one(j=j):
                value_t[:, j * rows : (j + 1) * rows] = jnp.transpose(value_win[j].astype(F32)).astype(BF16)

            pl.when(c >= j)(one)

    def part(s):
        off, wide = PIECES[s]
        heads = wide // HD
        return off // HD, heads, pl.ds(off // HD * rows, heads * rows), heads * rows

    def score(s):
        _, heads, span, n = part(s)

        def score_group(g, top):
            for u in range(GROUP):
                j = g * GROUP + u
                block = jnp.dot(key_win[j, :rows], q_t[:, span], preferred_element_type=F32)
                block = block + jnp.concatenate([bias[j]] * heads, axis=1)
                scores[j, :, span] = block
                top = jnp.maximum(top, jnp.max(block.reshape(rows // 8, 8, n), 0))
            return top

        top = lax.fori_loop(0, groups, score_group, jnp.full((8, n), HIDDEN, F32))
        return jnp.max(top, 0, keepdims=True) * EXP_SCALE

    def output(s, top):
        first, heads, span, n = part(s)
        out_t[:, :n] = jnp.zeros((HD, n), F32)

        def expo_group(g, total):
            ebs = []
            for u in range(GROUP):
                j = g * GROUP + u
                e = jnp.exp2(scores[j, :, span] * EXP_SCALE - top)
                eb = e.astype(BF16)
                expo[j, :, span] = eb
                ebs.append(eb)
                total = total + jnp.sum(e.reshape(rows // 8, 8, n), 0)
            keys = pl.ds(pl.multiple_of(g * GROUP * rows, rows), GROUP * rows)
            out_t[:, :n] += jnp.dot(
                value_t[:, keys], jnp.concatenate(ebs, axis=0), preferred_element_type=F32
            )
            return total

        total = lax.fori_loop(0, groups, expo_group, jnp.zeros((8, n), F32))
        inverse = 1.0 / jnp.sum(total, 0, keepdims=True)
        out_b = (out_t[:, :n] * inverse).astype(BF16).astype(F32)
        go = go_t[:, span].astype(F32)
        delta = jnp.sum(go * out_b, 0, keepdims=True) * inverse
        scaled = go * inverse
        gp_t[:, span] = scaled.astype(BF16)
        for i in range(heads):
            r = first + i
            attn[:, r * HD : (r + 1) * HD] = jnp.transpose(out_b[:, i * rows : (i + 1) * rows]).astype(BF16)
            gp_rows[r * rows : (r + 1) * rows] = jnp.transpose(scaled[:, i * rows : (i + 1) * rows]).astype(BF16)
        return delta

    def give(w, j, to, when):
        start(remote(
            pair_send.at[w, j], pair_recv.at[w, j], pair_ssem.at[w, j], pair_rsem.at[w, j], ctx=to,
        ), when)

    def take(w, j, into, when):
        def add_in():
            arrived(pair_recv.at[w, j], pair_rsem.at[w, j])
            pair_acc[w, into] += pair_recv[w, j].astype(F32)

        pl.when(when)(add_in)

    def give_sum(w, j):
        def store():
            pair_send[w, j] = pair_acc[w, j].astype(BF16)

        pl.when(c >= j)(store)
        give(w, j, jnp.maximum(c - j, 0), c >= j)

    def keep(w, j, value):
        if j % 4 == 0:
            pair_acc[w, j // 4 * 4] = value
        else:
            pair_send[w, j] = value.astype(BF16)

    def after_group(w, g):
        for j in reversed(range(g * GROUP, (g + 1) * GROUP)):
            if j % 4:
                give(w, j, z * 4 + lax.rem(y + 8 - j, 4), c >= j)

    def pair_second(w):
        for j in (7, 6, 5, 3, 2, 1):
            take(w, j, 4 * ((y + j) // 4), z * 4 + lax.rem(y + j, 4) >= j)
            if j == 5:
                give_sum(w, 8)
        give_sum(w, 4)

    def pair_third(w):
        for j in (8, 4):
            take(w, j, 0, z + j // 4 < rings)

    def backward_values():
        def group(g):
            for u in reversed(range(GROUP)):
                j = g * GROUP + u
                keep(1, j, jnp.dot(expo[j], gp_rows[...], preferred_element_type=F32))

        for g in reversed(range(WINDOW // GROUP + 1)):
            pl.when(g < groups)(functools.partial(group, g))
            after_group(1, g)

    def score_gradients(s, j, delta):
        _, _, span, _ = part(s)
        dp = jnp.dot(value_win[j], gp_t[:, span], preferred_element_type=F32)
        expo[j, :, span] = (expo[j, :, span].astype(F32) * (dp - delta)).astype(BF16)

    def backward_first(delta):
        @pl.loop(0, groups)
        def _(g):
            for u in range(GROUP):
                score_gradients(FIRST, g * GROUP + u, delta)

    def backward_keys(delta):
        def group(g):
            for u in reversed(range(GROUP)):
                j = g * GROUP + u
                score_gradients(SECOND, j, delta)
                keep(0, j, jnp.dot(expo[j], q_rows[...], preferred_element_type=F32) * SCALE)

        for g in reversed(range(WINDOW // GROUP + 1)):
            pl.when(g < groups)(functools.partial(group, g))
            after_group(0, g)

    def backward_queries(s):
        first, heads, span, n = part(s)
        dq_t[:, :n] = jnp.zeros((HD, n), F32)

        @pl.loop(0, groups)
        def _(g):
            keys = pl.ds(pl.multiple_of(g * GROUP * rows, rows), GROUP * rows)
            ds = jnp.concatenate([expo[g * GROUP + u, :, span] for u in range(GROUP)], axis=0)
            dq_t[:, :n] += jnp.dot(key_t[:, keys], ds, preferred_element_type=F32)

        inner = jnp.zeros((1, rows), F32)
        for i in range(heads):
            r = first + i
            one = dq_t[:, i * rows : (i + 1) * rows] * SCALE
            dproj[h, :, r * HD : (r + 1) * HD] = jnp.transpose(one).astype(BF16)
            inner += jnp.sum(one * q_t[:, r * rows : (r + 1) * rows].astype(F32), 0, keepdims=True)
        return inner

    def slot(ref, s, who, lo, size):
        off, wide = PIECES[s]
        return ref.at[who, pl.ds(lo, size), pl.ds(off, wide)]

    def move(s, n, who, lo, size, to):
        start(remote(slot(dproj, s, who, lo, size), slot(dproj, s, who, lo, size),
                     ag_send.at[s, n], ag_recv.at[s, n], head=to))

    def landed_piece(s, n, who, lo, size):
        arrived(slot(dproj, s, who, lo, size), ag_recv.at[s, n])

    def gather_send(s):
        for n, to in enumerate((right, left, far, partner)):
            move(s, n, h, 0, rows, to)

    def gather_pass(s):
        for n, who in enumerate((left, right, far)):
            landed_piece(s, n, who, 0, rows)
            move(s, 4 + n, who, 0, rows, partner)

    def add(s, who, fresh=False):
        off, wide = PIECES[s]
        value = lax.dot_general(
            dproj[who, :, off : off + wide], wv[who, :, off : off + wide],
            (((1,), (1,)), ((), ())), preferred_element_type=F32,
        )
        if fresh:
            dnormed[...] = value
        else:
            dnormed[...] += value

    def add_own(s, fresh=False):
        add(s, h, fresh)
        for who in (left, right, far):
            add(s, who)

    def add_rest(s):
        landed_piece(s, 3, partner, 0, rows)
        add(s, partner)
        for n, d in enumerate((3, 1, 2)):
            who = head_of(x + d, 1 - p)
            landed_piece(s, 4 + n, who, 0, rows)
            add(s, who)

    top_first = score(FIRST)
    queries(SECOND)
    top_second = score(SECOND)
    prepare_values()
    delta_first = output(FIRST, top_first)
    delta_second = output(SECOND, top_second)
    backward_values()
    backward_first(delta_first)
    inner = backward_queries(FIRST)
    gather_send(FIRST)
    backward_keys(delta_second)
    inner += backward_queries(SECOND)
    gather_send(SECOND)
    pair_second(1)
    gather_pass(FIRST)
    add_own(FIRST, True)
    pair_second(0)
    pair_third(1)
    dproj[h, :, PIECES[VALUES][0] :] = pair_acc[1, 0].astype(BF16)
    gather_send(VALUES)
    add_rest(FIRST)
    pair_third(0)
    dproj[h, :, PIECES[KEYS][0] : PIECES[VALUES][0]] = pair_acc[0, 0].astype(BF16)
    gather_send(KEYS)
    gather_pass(SECOND)
    prod = pair_acc[0, 0] * key_win[0, :rows].astype(F32) + pair_acc[1, 0] * value_win[0].astype(F32)
    inner += jnp.sum(jnp.transpose(prod), 0, keepdims=True)
    inner_stats[0] = jnp.broadcast_to(inner, (8, rows))
    small_first(inner_stats, in_send, in_recv)
    add_own(SECOND)
    add_rest(SECOND)
    gather_pass(VALUES)
    small_second(inner_stats, in_send, in_recv)
    add_own(VALUES)
    add_rest(VALUES)
    gather_pass(KEYS)
    add_own(KEYS)
    inner_col = small_total(inner_stats, in_recv)
    add_rest(KEYS)

    scale = recip[:, :1]
    weighted = tok[...].astype(F32) * scale
    gain_part = jnp.sum(dnormed[...] * weighted, 0, keepdims=True)
    lanes = wide_in // 128
    gain_stats[0] = jnp.zeros((8, 128), F32)
    for k in range(lanes):
        gain_stats[0, k : k + 1] = gain_part[:, k * 128 : (k + 1) * 128]
    for d in range(1, n_ctx):
        start(remote(
            gain_stats.at[0], gain_stats.at[d], gg_send.at[d], gg_recv.at[d], ctx=lax.rem(c + d, n_ctx),
        ))
    grad_tokens[...] = (
        dnormed[...] * gain[...].reshape(1, wide_in) * scale - weighted * (scale * inner_col * (1.0 / D))
    ).astype(BF16)
    gain_total = gain_stats[0]
    for d in range(1, n_ctx):
        arrived(gain_stats.at[d], gg_recv.at[d])
        gain_total = gain_total + gain_stats[d]
    grad_gain[...] = gain_total

    for copy, when in started:
        if when is None:
            copy.wait_send()
        else:
            pl.when(when)(copy.wait_send)


def hand_over(attn, grad_tokens, gain_rows, attn_out, grad_out, gain_out):
    attn_out[...] = attn[...]
    grad_out[...] = grad_tokens[...]
    wide = gain_out.shape[0]
    gain_out[...] = gain_rows[: wide // 128].reshape(wide)


def on_device(n_ctx, tokens, gain, qkv_weight, target, advantage, segment):
    rows, wide = tokens.shape
    group = qkv_weight.shape[1] // 8
    n = 3 * rows
    every = HEADS * rows
    slots = WINDOW + 1
    vmem = pl.BlockSpec(memory_space=pltpu.VMEM)
    anywhere = pl.BlockSpec(memory_space=pl.ANY)
    scratch = [
        ((rows, wide), BF16), ((8, wide, group), BF16),
        ((4, rows, group), BF16), ((4, rows, group), BF16), ((3, rows, group), BF16),
        ((2, rows // 2, group), F32), ((rows, group), F32),
        ((2, rows // 2, group), BF16), ((2, rows, group), BF16), ((2, rows, HD), BF16),
        ((6, 8, rows), F32), ((rows, HD), F32),
        ((slots, rows + 16, HD), BF16), ((slots, rows, HD), BF16),
        ((HD, slots * rows), BF16), ((HD, slots * rows), BF16), ((slots, rows, rows), F32),
        ((HEADS * rows, HD), BF16), ((HD, HEADS * rows), BF16), ((HD, HEADS * rows), BF16),
        ((slots, rows, every), F32), ((slots, rows, every), BF16), ((HD, n), F32),
        ((every, HD), BF16), ((HD, every), BF16), ((HD, n), F32),
        ((2, slots, rows, HD), F32), ((2, slots, rows, HD), BF16), ((2, slots, rows, HD), BF16),
        ((8, rows, group), BF16), ((6, 8, rows), F32), ((rows, wide), F32), ((n_ctx, 8, 128), F32),
    ]
    sems = [
        (4, 8), (4, 4), (4, 4), (4, 2), (4, 2), (4, 4), (4, 4), (4,), (4,),
        (2, 12), (2, slots), (2, slots), (2, slots),
        (4, 7), (4, 7), (4,), (4,), (n_ctx,), (n_ctx,),
    ]
    out_types = (
        jax.ShapeDtypeStruct((rows, HEADS * HD), BF16),
        jax.ShapeDtypeStruct((rows, wide), BF16),
    )
    out, grad_tokens, gain_rows = pl.pallas_call(
        functools.partial(kernel, n_ctx),
        out_shape=(*out_types, jax.ShapeDtypeStruct((8, 128), F32)),
        in_specs=[vmem, vmem, anywhere, vmem, vmem, vmem],
        out_specs=(vmem, vmem, vmem),
        scratch_shapes=[pltpu.VMEM(shape, dtype) for shape, dtype in scratch]
        + [pltpu.SemaphoreType.DMA(shape) for shape in sems],
        compiler_params=pltpu.CompilerParams(
            collective_id=0, has_side_effects=True, vmem_limit_bytes=60 * 1024 * 1024
        ),
    )(
        tokens, gain, qkv_weight, target,
        advantage.reshape(1, rows), segment.reshape(1, rows),
    )
    return pl.pallas_call(
        hand_over,
        out_shape=(*out_types, jax.ShapeDtypeStruct((wide,), F32)),
        in_specs=[vmem, vmem, vmem],
        out_specs=(vmem, vmem, vmem),
    )(out, grad_tokens, gain_rows)


def solution(mesh):
    placed = (P("ctx", "head"), P("head"), P("head", None), P("ctx", "head"), P("ctx"), P("ctx"))
    return jax.shard_map(
        functools.partial(on_device, mesh.shape["ctx"]),
        mesh=mesh,
        in_specs=placed,
        out_specs=(P("ctx", "head"), P("ctx", "head"), P("head")),
        check_vma=False,
    )
```

```python
import functools

import jax
import jax.numpy as jnp
from jax import lax
from jax.experimental import pallas as pl
from jax.experimental.pallas import tpu as pltpu
from jax.sharding import PartitionSpec as P

D = 5120
HD = 128
HEADS = 5
WINDOW = 8
EPSILON = 1e-06
SCALE = HD**-0.5
LOG2E = 1.4426950408889634
EXP_SCALE = SCALE * LOG2E
HIDDEN = -1e30
PIECES = ((640, 128), (768, 128), (0, 256), (256, 384))
KEYS, VALUES, FIRST, SECOND = range(4)
GROUP = 3
STEPS = (2, 1, 3, 0)
F32 = jnp.float32
BF16 = jnp.bfloat16


def kernel(
    n_ctx, tok, gain, w_hbm, target, advantage, segment,
    attn, grad_tokens, grad_gain,
    xb, wv, part_send, part_recv, chip_sum, hold, own, relay, landed, landed_far,
    stats, recip, key_win, value_win, key_t, value_t, bias,
    q_rows, q_t, go_t, scores, expo, out_t, gp_rows, gp_t, dq_t, pair_acc, pair_send, pair_recv,
    dproj, inner_stats, dnormed, gain_stats,
    w_sem, ps_send, ps_recv, r1_send, r1_recv, r2_send, r2_recv, st_send, st_recv,
    win_ssem, win_rsem, pair_ssem, pair_rsem,
    ag_send, ag_recv, in_send, in_recv, gg_send, gg_recv,
):
    rows, wide_in = tok.shape
    half = rows // 2
    c = lax.axis_index("ctx")
    h = lax.axis_index("head")
    x = h // 2
    p = lax.rem(h, 2)
    z = c // 4
    y = lax.rem(c, 4)
    rings = n_ctx // 4
    up, down = z * 4 + lax.rem(y + 1, 4), z * 4 + lax.rem(y + 3, 4)

    def head_of(xx, pp):
        return lax.rem(xx + 8, 4) * 2 + pp

    right, left, partner = head_of(x + 1, p), head_of(x - 1, p), head_of(x, 1 - p)
    far = head_of(x + 2, p)
    started = []

    def remote(src, dst, send, recv, **where):
        axis, index = next(iter(where.items()))
        return pltpu.make_async_remote_copy(
            src_ref=src, dst_ref=dst, send_sem=send, recv_sem=recv,
            device_id={axis: index}, device_id_type=pl.DeviceIdType.MESH,
        )

    def start(copy, when=None):
        started.append((copy, when))
        if when is None:
            copy.start()
        else:
            pl.when(when)(copy.start)

    def settle(copies):
        for copy, when in copies:
            if when is None:
                copy.wait_send()
            else:
                pl.when(when)(copy.wait_send)

    def arrived(dst, recv):
        remote(dst, dst, recv, recv, head=partner).wait_recv()

    def fetch(s, i):
        off, wide = PIECES[s]
        g = head_of(x + STEPS[i % 4], (1 - p) if i < 4 else p)
        first = pl.multiple_of(g * 896 + off, 128)
        return g, pltpu.make_async_copy(
            w_hbm.at[:, pl.ds(first, wide)], wv.at[g, :, pl.ds(off, wide)], w_sem.at[s, i]
        )

    for i in range(8):
        fetch(KEYS, i)[1].start()

    barrier = pltpu.get_barrier_semaphore()
    for other in (partner, right, left, head_of(x + 2, p)):
        pl.semaphore_signal(
            barrier, inc=1, device_id={"head": other}, device_id_type=pl.DeviceIdType.MESH
        )
    others = [lax.rem(c + d, n_ctx) for d in range(1, n_ctx)]
    for other in others:
        pl.semaphore_signal(
            barrier, inc=1, device_id={"ctx": other}, device_id_type=pl.DeviceIdType.MESH
        )

    for s in range(1, 4):
        for i in range(8):
            fetch(s, i)[1].start()

    gain_row = gain[...].reshape(1, wide_in)
    features = tok[...].astype(F32)
    xb[...] = (features * gain_row).astype(BF16)
    squares = jnp.sum(features * features, -1, keepdims=True)
    stats[0] = jnp.transpose(jnp.broadcast_to(squares, (rows, HD)))[:8]

    def project(s):
        off, wide = PIECES[s]
        cols = pl.ds(off, wide)
        for i in range(4):
            g, copy = fetch(s, i)
            copy.wait()
            part_send[i, :, off : off + wide] = jnp.dot(
                xb[...], wv[g, :, off : off + wide], preferred_element_type=F32
            ).astype(BF16)
            if s == 0 and i == 0:
                pl.semaphore_wait(barrier, 4 + len(others))
                small_first(stats, st_send, st_recv)
            start(remote(
                part_send.at[i, :, cols], part_recv.at[i, :, cols],
                ps_send.at[s, i], ps_recv.at[s, i], head=partner,
            ))
        if s == KEYS:
            small_second(stats, st_send, st_recv)
        for i in range(4):
            g, copy = fetch(s, 4 + i)
            copy.wait()
            mine = jnp.dot(xb[...], wv[g, :, off : off + wide], preferred_element_type=F32)
            arrived(part_recv.at[i, :, cols], ps_recv.at[s, i])
            mine = mine + part_recv[i, :, off : off + wide].astype(F32)
            if i < 3:
                chip_sum[i, :, off : off + wide] = mine.astype(BF16)
            top = pl.ds(0, half)
            low = pl.ds(half, half)
            if s < 2 and i < 3:
                start(remote(
                    chip_sum.at[i, :, cols], (landed_far.at[s], landed.at[0, :, cols], landed.at[1, :, cols])[i],
                    r2_send.at[s, i], r2_recv.at[s, i], head=(far, right, left)[i],
                ))
            elif i == 0:
                start(remote(
                    chip_sum.at[0, top, cols], relay.at[0, :, cols],
                    r1_send.at[s, 0], r1_recv.at[s, 0], head=right,
                ))
                start(remote(
                    chip_sum.at[0, low, cols], relay.at[1, :, cols],
                    r1_send.at[s, 1], r1_recv.at[s, 1], head=left,
                ))
            elif i == 1:
                hold[0, :, off : off + wide] = mine[:half]
                start(remote(
                    chip_sum.at[1, low, cols], landed.at[0, low, cols],
                    r2_send.at[s, 0], r2_recv.at[s, 0], head=right,
                ))
            elif i == 2:
                hold[1, :, off : off + wide] = mine[half:]
                start(remote(
                    chip_sum.at[2, top, cols], landed.at[1, top, cols],
                    r2_send.at[s, 1], r2_recv.at[s, 1], head=left,
                ))
            else:
                own[:, off : off + wide] = mine

    def pass_on(s):
        off, wide = PIECES[s]
        cols = pl.ds(off, wide)
        top = pl.ds(0, half)
        low = pl.ds(half, half)
        arrived(relay.at[0, :, cols], r1_recv.at[s, 0])
        chip_sum[1, :half, off : off + wide] = (
            hold[0, :, off : off + wide] + relay[0, :, off : off + wide].astype(F32)
        ).astype(BF16)
        start(remote(
            chip_sum.at[1, top, cols], landed.at[0, top, cols],
            r2_send.at[s, 2], r2_recv.at[s, 2], head=right,
        ))
        arrived(relay.at[1, :, cols], r1_recv.at[s, 1])
        chip_sum[2, half:, off : off + wide] = (
            hold[1, :, off : off + wide] + relay[1, :, off : off + wide].astype(F32)
        ).astype(BF16)
        start(remote(
            chip_sum.at[2, low, cols], landed.at[1, low, cols],
            r2_send.at[s, 3], r2_recv.at[s, 3], head=left,
        ))

    def finish(s):
        off, wide = PIECES[s]
        cols = pl.ds(off, wide)
        top = pl.ds(0, half)
        low = pl.ds(half, half)
        if s < 2:
            arrived(landed_far.at[s], r2_recv.at[s, 0])
            arrived(landed.at[0, :, cols], r2_recv.at[s, 1])
            arrived(landed.at[1, :, cols], r2_recv.at[s, 2])
        else:
            arrived(landed.at[0, low, cols], r2_recv.at[s, 0])
            arrived(landed.at[1, top, cols], r2_recv.at[s, 1])
            arrived(landed.at[0, top, cols], r2_recv.at[s, 2])
            arrived(landed.at[1, low, cols], r2_recv.at[s, 3])
        total = own[:, off : off + wide] + landed[0, :, off : off + wide].astype(F32)
        total = total + landed[1, :, off : off + wide].astype(F32)
        if s < 2:
            total = total + landed_far[s].astype(F32)
        scale = recip[:, :1]
        return (total * scale).astype(BF16)

    def small_first(ref, send, recv):
        start(remote(ref.at[0], ref.at[1], send.at[0], recv.at[0], head=partner))

    def small_second(ref, send, recv):
        arrived(ref.at[1], recv.at[0])
        ref[2] = ref[0] + ref[1]
        for d in range(1, 4):
            start(remote(ref.at[2], ref.at[2 + d], send.at[d], recv.at[d], head=head_of(x + d, p)))

    def small_total(ref, recv):
        for d in range(1, 4):
            arrived(ref.at[2 + d], recv.at[d])
        return jnp.transpose(ref[2] + ref[3] + ref[4] + ref[5])[:, :1]

    project(KEYS)
    project(VALUES)
    seg_row = segment[...].astype(F32)
    which = lax.broadcasted_iota(jnp.int32, (16, HD), 0)
    seg_block = jnp.zeros((16, HD), F32)
    for k in range(rows // HD):
        seg_block = jnp.where(which == k, seg_row[:, k * HD : (k + 1) * HD], seg_block)
    key_win[0, rows:] = seg_block.astype(BF16)
    project(FIRST)
    recip[...] = jnp.broadcast_to(
        lax.rsqrt(small_total(stats, st_recv) / D + EPSILON), (rows, HD)
    )

    windows = (key_win, value_win)

    def share(w, n, src, dst, to, when):
        start(remote(
            windows[w].at[src], windows[w].at[dst], win_ssem.at[w, n], win_rsem.at[w, dst], ctx=to,
        ), when)

    def here(w, j):
        pl.when(c >= j)(lambda: arrived(windows[w].at[j], win_rsem.at[w, j]))

    def share_first(w):
        for d in (1, 2):
            share(w, d, 0, 4 * d, jnp.minimum(c + 4 * d, n_ctx - 1), z + d < rings)
        for d in range(1, 4):
            share(w, 2 + d, 0, d, z * 4 + jnp.minimum(y + d, 3), y + d <= 3)

    def share_second(w):
        here(w, 4)
        for d in (1, 3, 2):
            share(w, 5 + d, 4, 4 + d - 4 * ((y + d) // 4), z * 4 + lax.rem(y + d, 4), z >= 1)

    def share_third(w):
        here(w, 8)
        for d in range(1, 4):
            share(w, 8 + d, 8, 8 - d, z * 4 + jnp.maximum(y - d, 0), (z >= 2) & (y >= d))

    def share_last(w):
        for j in (1, 2, 3, 5, 6, 7):
            here(w, j)

    key_win[0, :rows] = finish(KEYS)
    share_first(0)
    project(SECOND)
    value_win[0] = finish(VALUES)
    share_first(1)
    pass_on(FIRST)
    share_second(0)
    share_third(0)
    share_second(1)
    share_third(1)
    pass_on(SECOND)

    factor = 0.25 * advantage[...].astype(F32)
    for r in range(HEADS):
        block = jnp.transpose(target[:, r * HD : (r + 1) * HD].astype(F32))
        go_t[:, r * rows : (r + 1) * rows] = (block * factor).astype(BF16)

    def queries(s):
        q = finish(s)
        first = PIECES[s][0] // HD
        for i in range(PIECES[s][1] // HD):
            one = q[:, i * HD : (i + 1) * HD]
            q_rows[(first + i) * rows : (first + i + 1) * rows] = one
            q_t[:, (first + i) * rows : (first + i + 1) * rows] = jnp.transpose(one.astype(F32)).astype(BF16)

    queries(FIRST)
    share_last(0)

    blocks = jnp.minimum(c, WINDOW) + 1
    groups = (blocks + GROUP - 1) // GROUP

    def prepare_keys(j, diagonal):
        key_t[:, pl.ds(pl.multiple_of(j * rows, rows), rows)] = (
            jnp.transpose(key_win[j, :rows].astype(F32)).astype(BF16)
        )
        ids = jnp.transpose(key_win[j, rows:].astype(F32))
        for k in range(rows // HD):
            visible = ids[:, k : k + 1] == seg_row
            if diagonal:
                k_pos = lax.broadcasted_iota(jnp.int32, (HD, rows), 0) + k * HD
                q_pos = lax.broadcasted_iota(jnp.int32, (HD, rows), 1)
                visible = visible & (k_pos <= q_pos)
            bias[j, k * HD : (k + 1) * HD] = jnp.where(visible, 0.0, HIDDEN)

    prepare_keys(0, True)

    @pl.loop(1, blocks)
    def _(j):
        prepare_keys(j, False)

    @pl.loop(blocks, groups * GROUP)
    def _(j):
        span = pl.ds(pl.multiple_of(j * rows, rows), rows)
        key_win[j] = jnp.zeros((rows + 16, HD), BF16)
        value_win[j] = jnp.zeros((rows, HD), BF16)
        key_t[:, span] = jnp.zeros((HD, rows), BF16)
        value_t[:, span] = jnp.zeros((HD, rows), BF16)
        bias[j] = jnp.full((rows, rows), HIDDEN, F32)

    def prepare_values():
        for j in (0, 4, 1, 2, 3, 8, 5, 6, 7):
            if j % 4:
                here(1, j)

            def one(j=j):
                value_t[:, j * rows : (j + 1) * rows] = jnp.transpose(value_win[j].astype(F32)).astype(BF16)

            pl.when(c >= j)(one)

    def part(s):
        off, wide = PIECES[s]
        heads = wide // HD
        return off // HD, heads, pl.ds(off // HD * rows, heads * rows), heads * rows

    def score(s):
        _, heads, span, n = part(s)

        def score_group(g, top):
            for u in range(GROUP):
                j = g * GROUP + u
                block = jnp.dot(key_win[j, :rows], q_t[:, span], preferred_element_type=F32)
                block = block + jnp.concatenate([bias[j]] * heads, axis=1)
                scores[j, :, span] = block
                top = jnp.maximum(top, jnp.max(block.reshape(rows // 8, 8, n), 0))
            return top

        top = lax.fori_loop(0, groups, score_group, jnp.full((8, n), HIDDEN, F32))
        return jnp.max(top, 0, keepdims=True) * EXP_SCALE

    def output(s, top):
        first, heads, span, n = part(s)
        out_t[:, :n] = jnp.zeros((HD, n), F32)

        def expo_group(g, total):
            ebs = []
            for u in range(GROUP):
                j = g * GROUP + u
                e = jnp.exp2(scores[j, :, span] * EXP_SCALE - top)
                eb = e.astype(BF16)
                expo[j, :, span] = eb
                ebs.append(eb)
                total = total + jnp.sum(e.reshape(rows // 8, 8, n), 0)
            keys = pl.ds(pl.multiple_of(g * GROUP * rows, rows), GROUP * rows)
            out_t[:, :n] += jnp.dot(
                value_t[:, keys], jnp.concatenate(ebs, axis=0), preferred_element_type=F32
            )
            return total

        total = lax.fori_loop(0, groups, expo_group, jnp.zeros((8, n), F32))
        inverse = 1.0 / jnp.sum(total, 0, keepdims=True)
        out_b = (out_t[:, :n] * inverse).astype(BF16).astype(F32)
        go = go_t[:, span].astype(F32)
        delta = jnp.sum(go * out_b, 0, keepdims=True) * inverse
        scaled = go * inverse
        gp_t[:, span] = scaled.astype(BF16)
        for i in range(heads):
            r = first + i
            attn[:, r * HD : (r + 1) * HD] = jnp.transpose(out_b[:, i * rows : (i + 1) * rows]).astype(BF16)
            gp_rows[r * rows : (r + 1) * rows] = jnp.transpose(scaled[:, i * rows : (i + 1) * rows]).astype(BF16)
        return delta

    def give(w, j, to, when):
        start(remote(
            pair_send.at[w, j], pair_recv.at[w, j], pair_ssem.at[w, j], pair_rsem.at[w, j], ctx=to,
        ), when)

    def take(w, j, into, when):
        def add_in():
            arrived(pair_recv.at[w, j], pair_rsem.at[w, j])
            pair_acc[w, into] += pair_recv[w, j].astype(F32)

        pl.when(when)(add_in)

    def give_sum(w, j):
        def store():
            pair_send[w, j] = pair_acc[w, j].astype(BF16)

        pl.when(c >= j)(store)
        give(w, j, jnp.maximum(c - j, 0), c >= j)

    def keep(w, j, value):
        if j % 4 == 0:
            pair_acc[w, j // 4 * 4] = value
        else:
            pair_send[w, j] = value.astype(BF16)

    def after_group(w, g):
        for j in reversed(range(g * GROUP, (g + 1) * GROUP)):
            if j % 4:
                give(w, j, z * 4 + lax.rem(y + 8 - j, 4), c >= j)

    def pair_second(w):
        for j in (7, 6, 5, 3, 2, 1):
            take(w, j, 4 * ((y + j) // 4), z * 4 + lax.rem(y + j, 4) >= j)
            if j == 5:
                give_sum(w, 8)
        give_sum(w, 4)

    def pair_third(w):
        for j in (8, 4):
            take(w, j, 0, z + j // 4 < rings)

    def backward_values():
        later = part(SECOND)[2]

        def group(g):
            for u in reversed(range(GROUP)):
                j = g * GROUP + u
                dv = jnp.dot(expo[j, :, later], gp_rows[later], preferred_element_type=F32)
                keep(1, j, pair_acc[1, j] + dv)

        for g in reversed(range(WINDOW // GROUP + 1)):
            pl.when(g < groups)(functools.partial(group, g))
            after_group(1, g)

    def score_gradients(s, j, delta):
        _, _, span, _ = part(s)
        dp = jnp.dot(value_win[j], gp_t[:, span], preferred_element_type=F32)
        expo[j, :, span] = (expo[j, :, span].astype(F32) * (dp - delta)).astype(BF16)

    def backward_first(delta):
        sooner = part(FIRST)[2]

        @pl.loop(0, groups)
        def _(g):
            for u in range(GROUP):
                j = g * GROUP + u
                pair_acc[1, j] = jnp.dot(expo[j, :, sooner], gp_rows[sooner], preferred_element_type=F32)
                score_gradients(FIRST, j, delta)

    def backward_keys(delta):
        def group(g):
            for u in reversed(range(GROUP)):
                j = g * GROUP + u
                score_gradients(SECOND, j, delta)
                keep(0, j, jnp.dot(expo[j], q_rows[...], preferred_element_type=F32) * SCALE)

        for g in reversed(range(WINDOW // GROUP + 1)):
            pl.when(g < groups)(functools.partial(group, g))
            after_group(0, g)

    def backward_queries(s):
        first, heads, span, n = part(s)
        dq_t[:, :n] = jnp.zeros((HD, n), F32)

        @pl.loop(0, groups)
        def _(g):
            keys = pl.ds(pl.multiple_of(g * GROUP * rows, rows), GROUP * rows)
            ds = jnp.concatenate([expo[g * GROUP + u, :, span] for u in range(GROUP)], axis=0)
            dq_t[:, :n] += jnp.dot(key_t[:, keys], ds, preferred_element_type=F32)

        inner = jnp.zeros((1, rows), F32)
        for i in range(heads):
            r = first + i
            one = dq_t[:, i * rows : (i + 1) * rows] * SCALE
            dproj[h, :, r * HD : (r + 1) * HD] = jnp.transpose(one).astype(BF16)
            inner += jnp.sum(one * q_t[:, r * rows : (r + 1) * rows].astype(F32), 0, keepdims=True)
        return inner

    def slot(ref, s, who, lo, size):
        off, wide = PIECES[s]
        return ref.at[who, pl.ds(lo, size), pl.ds(off, wide)]

    def move(s, n, who, lo, size, to):
        start(remote(slot(dproj, s, who, lo, size), slot(dproj, s, who, lo, size),
                     ag_send.at[s, n], ag_recv.at[s, n], head=to))

    def landed_piece(s, n, who, lo, size):
        arrived(slot(dproj, s, who, lo, size), ag_recv.at[s, n])

    def gather_send(s):
        for n, to in ((3, partner), (2, far), (0, right), (1, left)):
            move(s, n, h, 0, rows, to)

    def gather_pass(s):
        for n, who in enumerate((left, right, far)):
            landed_piece(s, n, who, 0, rows)
            move(s, 4 + n, who, 0, rows, partner)

    def add(s, who, fresh=False):
        off, wide = PIECES[s]
        value = lax.dot_general(
            dproj[who, :, off : off + wide], wv[who, :, off : off + wide],
            (((1,), (1,)), ((), ())), preferred_element_type=F32,
        )
        if fresh:
            dnormed[...] = value
        else:
            dnormed[...] += value

    def add_own(s, fresh=False):
        add(s, h, fresh)
        for who in (left, right, far):
            add(s, who)

    def add_rest(s):
        landed_piece(s, 3, partner, 0, rows)
        add(s, partner)
        for n, d in enumerate((3, 1, 2)):
            who = head_of(x + d, 1 - p)
            landed_piece(s, 4 + n, who, 0, rows)
            add(s, who)

    top_first = score(FIRST)
    queries(SECOND)
    top_second = score(SECOND)
    prepare_values()
    delta_first = output(FIRST, top_first)
    backward_first(delta_first)
    inner = backward_queries(FIRST)
    gather_send(FIRST)
    delta_second = output(SECOND, top_second)
    backward_values()
    backward_keys(delta_second)
    inner += backward_queries(SECOND)
    gather_send(SECOND)
    pair_second(1)
    gather_pass(FIRST)
    add_own(FIRST, True)
    pair_second(0)
    pair_third(1)
    dproj[h, :, PIECES[VALUES][0] :] = pair_acc[1, 0].astype(BF16)
    gather_send(VALUES)
    add_rest(FIRST)
    pair_third(0)
    dproj[h, :, PIECES[KEYS][0] : PIECES[VALUES][0]] = pair_acc[0, 0].astype(BF16)
    gather_send(KEYS)
    gather_pass(SECOND)
    prod = pair_acc[0, 0] * key_win[0, :rows].astype(F32) + pair_acc[1, 0] * value_win[0].astype(F32)
    inner += jnp.sum(jnp.transpose(prod), 0, keepdims=True)
    inner_stats[0] = jnp.broadcast_to(inner, (8, rows))
    small_first(inner_stats, in_send, in_recv)
    add_own(SECOND)
    add_rest(SECOND)
    gather_pass(VALUES)
    small_second(inner_stats, in_send, in_recv)
    add_own(VALUES)
    add_rest(VALUES)
    gather_pass(KEYS)
    add_own(KEYS)
    inner_col = small_total(inner_stats, in_recv)
    add_rest(KEYS)

    scale = recip[:, :1]
    weighted = tok[...].astype(F32) * scale
    gain_part = jnp.sum(dnormed[...] * weighted, 0, keepdims=True)
    lanes = wide_in // 128
    gain_stats[0] = jnp.zeros((8, 128), F32)
    for k in range(lanes):
        gain_stats[0, k : k + 1] = gain_part[:, k * 128 : (k + 1) * 128]
    before = len(started)
    for d in range(1, n_ctx):
        start(remote(
            gain_stats.at[0], gain_stats.at[d], gg_send.at[d], gg_recv.at[d], ctx=lax.rem(c + d, n_ctx),
        ))
    grad_tokens[...] = (
        dnormed[...] * gain[...].reshape(1, wide_in) * scale - weighted * (scale * inner_col * (1.0 / D))
    ).astype(BF16)
    settle(started[:before])
    gain_total = gain_stats[0]
    for d in range(1, n_ctx):
        arrived(gain_stats.at[d], gg_recv.at[d])
        gain_total = gain_total + gain_stats[d]
    grad_gain[...] = gain_total

    settle(started[before:])


def hand_over(attn, grad_tokens, gain_rows, attn_out, grad_out, gain_out):
    attn_out[...] = attn[...]
    grad_out[...] = grad_tokens[...]
    wide = gain_out.shape[0]
    gain_out[...] = gain_rows[: wide // 128].reshape(wide)


def on_device(n_ctx, tokens, gain, qkv_weight, target, advantage, segment):
    rows, wide = tokens.shape
    group = qkv_weight.shape[1] // 8
    n = 3 * rows
    every = HEADS * rows
    slots = WINDOW + 1
    vmem = pl.BlockSpec(memory_space=pltpu.VMEM)
    anywhere = pl.BlockSpec(memory_space=pl.ANY)
    scratch = [
        ((rows, wide), BF16), ((8, wide, group), BF16),
        ((4, rows, group), BF16), ((4, rows, group), BF16), ((3, rows, group), BF16),
        ((2, rows // 2, group), F32), ((rows, group), F32),
        ((2, rows // 2, group), BF16), ((2, rows, group), BF16), ((2, rows, HD), BF16),
        ((6, 8, rows), F32), ((rows, HD), F32),
        ((slots, rows + 16, HD), BF16), ((slots, rows, HD), BF16),
        ((HD, slots * rows), BF16), ((HD, slots * rows), BF16), ((slots, rows, rows), F32),
        ((HEADS * rows, HD), BF16), ((HD, HEADS * rows), BF16), ((HD, HEADS * rows), BF16),
        ((slots, rows, every), F32), ((slots, rows, every), BF16), ((HD, n), F32),
        ((every, HD), BF16), ((HD, every), BF16), ((HD, n), F32),
        ((2, slots, rows, HD), F32), ((2, slots, rows, HD), BF16), ((2, slots, rows, HD), BF16),
        ((8, rows, group), BF16), ((6, 8, rows), F32), ((rows, wide), F32), ((n_ctx, 8, 128), F32),
    ]
    sems = [
        (4, 8), (4, 4), (4, 4), (4, 2), (4, 2), (4, 4), (4, 4), (4,), (4,),
        (2, 12), (2, slots), (2, slots), (2, slots),
        (4, 7), (4, 7), (4,), (4,), (n_ctx,), (n_ctx,),
    ]
    out_types = (
        jax.ShapeDtypeStruct((rows, HEADS * HD), BF16),
        jax.ShapeDtypeStruct((rows, wide), BF16),
    )
    out, grad_tokens, gain_rows = pl.pallas_call(
        functools.partial(kernel, n_ctx),
        out_shape=(*out_types, jax.ShapeDtypeStruct((8, 128), F32)),
        in_specs=[vmem, vmem, anywhere, vmem, vmem, vmem],
        out_specs=(vmem, vmem, vmem),
        scratch_shapes=[pltpu.VMEM(shape, dtype) for shape, dtype in scratch]
        + [pltpu.SemaphoreType.DMA(shape) for shape in sems],
        compiler_params=pltpu.CompilerParams(
            collective_id=0, has_side_effects=True, vmem_limit_bytes=60 * 1024 * 1024
        ),
    )(
        tokens, gain, qkv_weight, target,
        advantage.reshape(1, rows), segment.reshape(1, rows),
    )
    return pl.pallas_call(
        hand_over,
        out_shape=(*out_types, jax.ShapeDtypeStruct((wide,), F32)),
        in_specs=[vmem, vmem, vmem],
        out_specs=(vmem, vmem, vmem),
    )(out, grad_tokens, gain_rows)


def solution(mesh):
    placed = (P("ctx", "head"), P("head"), P("head", None), P("ctx", "head"), P("ctx"), P("ctx"))
    return jax.shard_map(
        functools.partial(on_device, mesh.shape["ctx"]),
        mesh=mesh,
        in_specs=placed,
        out_specs=(P("ctx", "head"), P("ctx", "head"), P("head")),
        check_vma=False,
    )
```

```python
import functools

import jax
import jax.numpy as jnp
from jax import lax
from jax.experimental import pallas as pl
from jax.experimental.pallas import tpu as pltpu
from jax.sharding import PartitionSpec as P

D = 5120
HD = 128
HEADS = 5
WINDOW = 8
EPSILON = 1e-06
SCALE = HD**-0.5
LOG2E = 1.4426950408889634
EXP_SCALE = SCALE * LOG2E
HIDDEN = -1e30
PIECES = ((640, 128), (768, 128), (0, 256), (256, 384))
KEYS, VALUES, FIRST, SECOND = range(4)
GROUP = 3
STEPS = (2, 1, 3, 0)
F32 = jnp.float32
BF16 = jnp.bfloat16


def kernel(
    n_ctx, tok, gain, w_hbm, target, advantage, segment,
    attn, grad_tokens, grad_gain,
    xb, wv, part_send, part_recv, chip_sum, hold, own, relay, landed, landed_far,
    stats, recip, key_win, value_win, key_t, value_t, bias,
    q_rows, q_t, go_t, scores, expo, out_t, gp_rows, gp_t, dq_t, pair_acc, pair_send, pair_recv,
    dproj, inner_stats, dnormed, gain_stats,
    w_sem, ps_send, ps_recv, r1_send, r1_recv, r2_send, r2_recv, st_send, st_recv,
    win_ssem, win_rsem, pair_ssem, pair_rsem,
    ag_send, ag_recv, in_send, in_recv, gg_send, gg_recv,
):
    rows, wide_in = tok.shape
    half = rows // 2
    c = lax.axis_index("ctx")
    h = lax.axis_index("head")
    x = h // 2
    p = lax.rem(h, 2)
    z = c // 4
    y = lax.rem(c, 4)
    rings = n_ctx // 4
    up, down = z * 4 + lax.rem(y + 1, 4), z * 4 + lax.rem(y + 3, 4)

    def head_of(xx, pp):
        return lax.rem(xx + 8, 4) * 2 + pp

    right, left, partner = head_of(x + 1, p), head_of(x - 1, p), head_of(x, 1 - p)
    far = head_of(x + 2, p)
    started = []

    def remote(src, dst, send, recv, **where):
        axis, index = next(iter(where.items()))
        return pltpu.make_async_remote_copy(
            src_ref=src, dst_ref=dst, send_sem=send, recv_sem=recv,
            device_id={axis: index}, device_id_type=pl.DeviceIdType.MESH,
        )

    def start(copy, when=None):
        started.append((copy, when))
        if when is None:
            copy.start()
        else:
            pl.when(when)(copy.start)

    def settle(copies):
        for copy, when in copies:
            if when is None:
                copy.wait_send()
            else:
                pl.when(when)(copy.wait_send)

    def arrived(dst, recv):
        remote(dst, dst, recv, recv, head=partner).wait_recv()

    def fetch(s, i):
        off, wide = PIECES[s]
        g = head_of(x + STEPS[i % 4], (1 - p) if i < 4 else p)
        first = pl.multiple_of(g * 896 + off, 128)
        return g, pltpu.make_async_copy(
            w_hbm.at[:, pl.ds(first, wide)], wv.at[g, :, pl.ds(off, wide)], w_sem.at[s, i]
        )

    for i in range(8):
        fetch(KEYS, i)[1].start()

    barrier = pltpu.get_barrier_semaphore()
    for other in (partner, right, left, head_of(x + 2, p)):
        pl.semaphore_signal(
            barrier, inc=1, device_id={"head": other}, device_id_type=pl.DeviceIdType.MESH
        )
    others = [lax.rem(c + d, n_ctx) for d in range(1, n_ctx)]
    for other in others:
        pl.semaphore_signal(
            barrier, inc=1, device_id={"ctx": other}, device_id_type=pl.DeviceIdType.MESH
        )

    for s in range(1, 4):
        for i in range(8):
            fetch(s, i)[1].start()

    gain_row = gain[...].reshape(1, wide_in)
    features = tok[...].astype(F32)
    xb[...] = (features * gain_row).astype(BF16)
    squares = jnp.sum(features * features, -1, keepdims=True)
    stats[0] = jnp.transpose(jnp.broadcast_to(squares, (rows, HD)))[:8]

    def project(s):
        off, wide = PIECES[s]
        cols = pl.ds(off, wide)
        for i in range(4):
            g, copy = fetch(s, i)
            copy.wait()
            part_send[i, :, off : off + wide] = jnp.dot(
                xb[...], wv[g, :, off : off + wide], preferred_element_type=F32
            ).astype(BF16)
            if s == 0 and i == 0:
                pl.semaphore_wait(barrier, 4 + len(others))
                small_first(stats, st_send, st_recv)
            start(remote(
                part_send.at[i, :, cols], part_recv.at[i, :, cols],
                ps_send.at[s, i], ps_recv.at[s, i], head=partner,
            ))
        if s == KEYS:
            small_second(stats, st_send, st_recv)
        for i in range(4):
            g, copy = fetch(s, 4 + i)
            copy.wait()
            mine = jnp.dot(xb[...], wv[g, :, off : off + wide], preferred_element_type=F32)
            arrived(part_recv.at[i, :, cols], ps_recv.at[s, i])
            mine = mine + part_recv[i, :, off : off + wide].astype(F32)
            if i < 3:
                chip_sum[i, :, off : off + wide] = mine.astype(BF16)
            top = pl.ds(0, half)
            low = pl.ds(half, half)
            if s < 2 and i < 3:
                start(remote(
                    chip_sum.at[i, :, cols], (landed_far.at[s], landed.at[0, :, cols], landed.at[1, :, cols])[i],
                    r2_send.at[s, i], r2_recv.at[s, i], head=(far, right, left)[i],
                ))
            elif i == 0:
                start(remote(
                    chip_sum.at[0, top, cols], relay.at[0, :, cols],
                    r1_send.at[s, 0], r1_recv.at[s, 0], head=right,
                ))
                start(remote(
                    chip_sum.at[0, low, cols], relay.at[1, :, cols],
                    r1_send.at[s, 1], r1_recv.at[s, 1], head=left,
                ))
            elif i == 1:
                hold[0, :, off : off + wide] = mine[:half]
                start(remote(
                    chip_sum.at[1, low, cols], landed.at[0, low, cols],
                    r2_send.at[s, 0], r2_recv.at[s, 0], head=right,
                ))
            elif i == 2:
                hold[1, :, off : off + wide] = mine[half:]
                start(remote(
                    chip_sum.at[2, top, cols], landed.at[1, top, cols],
                    r2_send.at[s, 1], r2_recv.at[s, 1], head=left,
                ))
            else:
                own[:, off : off + wide] = mine

    def pass_on(s):
        off, wide = PIECES[s]
        cols = pl.ds(off, wide)
        top = pl.ds(0, half)
        low = pl.ds(half, half)
        arrived(relay.at[0, :, cols], r1_recv.at[s, 0])
        chip_sum[1, :half, off : off + wide] = (
            hold[0, :, off : off + wide] + relay[0, :, off : off + wide].astype(F32)
        ).astype(BF16)
        start(remote(
            chip_sum.at[1, top, cols], landed.at[0, top, cols],
            r2_send.at[s, 2], r2_recv.at[s, 2], head=right,
        ))
        arrived(relay.at[1, :, cols], r1_recv.at[s, 1])
        chip_sum[2, half:, off : off + wide] = (
            hold[1, :, off : off + wide] + relay[1, :, off : off + wide].astype(F32)
        ).astype(BF16)
        start(remote(
            chip_sum.at[2, low, cols], landed.at[1, low, cols],
            r2_send.at[s, 3], r2_recv.at[s, 3], head=left,
        ))

    def finish(s):
        off, wide = PIECES[s]
        cols = pl.ds(off, wide)
        top = pl.ds(0, half)
        low = pl.ds(half, half)
        if s < 2:
            arrived(landed_far.at[s], r2_recv.at[s, 0])
            arrived(landed.at[0, :, cols], r2_recv.at[s, 1])
            arrived(landed.at[1, :, cols], r2_recv.at[s, 2])
        else:
            arrived(landed.at[0, low, cols], r2_recv.at[s, 0])
            arrived(landed.at[1, top, cols], r2_recv.at[s, 1])
            arrived(landed.at[0, top, cols], r2_recv.at[s, 2])
            arrived(landed.at[1, low, cols], r2_recv.at[s, 3])
        total = own[:, off : off + wide] + landed[0, :, off : off + wide].astype(F32)
        total = total + landed[1, :, off : off + wide].astype(F32)
        if s < 2:
            total = total + landed_far[s].astype(F32)
        scale = recip[:, :1]
        return (total * scale).astype(BF16)

    def small_first(ref, send, recv):
        start(remote(ref.at[0], ref.at[1], send.at[0], recv.at[0], head=partner))

    def small_second(ref, send, recv):
        arrived(ref.at[1], recv.at[0])
        ref[2] = ref[0] + ref[1]
        for d in range(1, 4):
            start(remote(ref.at[2], ref.at[2 + d], send.at[d], recv.at[d], head=head_of(x + d, p)))

    def small_total(ref, recv):
        for d in range(1, 4):
            arrived(ref.at[2 + d], recv.at[d])
        return jnp.transpose(ref[2] + ref[3] + ref[4] + ref[5])[:, :1]

    project(KEYS)
    project(VALUES)
    seg_row = segment[...].astype(F32)
    which = lax.broadcasted_iota(jnp.int32, (16, HD), 0)
    seg_block = jnp.zeros((16, HD), F32)
    for k in range(rows // HD):
        seg_block = jnp.where(which == k, seg_row[:, k * HD : (k + 1) * HD], seg_block)
    key_win[0, rows:] = seg_block.astype(BF16)
    project(FIRST)
    recip[...] = jnp.broadcast_to(
        lax.rsqrt(small_total(stats, st_recv) / D + EPSILON), (rows, HD)
    )

    windows = (key_win, value_win)

    def share(w, n, src, dst, to, when):
        start(remote(
            windows[w].at[src], windows[w].at[dst], win_ssem.at[w, n], win_rsem.at[w, dst], ctx=to,
        ), when)

    def here(w, j):
        pl.when(c >= j)(lambda: arrived(windows[w].at[j], win_rsem.at[w, j]))

    def share_first(w):
        for d in (1, 2):
            share(w, d, 0, 4 * d, jnp.minimum(c + 4 * d, n_ctx - 1), z + d < rings)
        for d in range(1, 4):
            share(w, 2 + d, 0, d, z * 4 + jnp.minimum(y + d, 3), y + d <= 3)

    def share_second(w):
        here(w, 4)
        for d in (1, 3, 2):
            share(w, 5 + d, 4, 4 + d - 4 * ((y + d) // 4), z * 4 + lax.rem(y + d, 4), z >= 1)

    def share_third(w):
        here(w, 8)
        for d in range(1, 4):
            share(w, 8 + d, 8, 8 - d, z * 4 + jnp.maximum(y - d, 0), (z >= 2) & (y >= d))

    def share_last(w):
        for j in (1, 2, 3, 5, 6, 7):
            here(w, j)

    key_win[0, :rows] = finish(KEYS)
    share_first(0)
    project(SECOND)
    value_win[0] = finish(VALUES)
    share_first(1)
    pass_on(FIRST)
    share_second(0)
    share_third(0)
    share_second(1)
    share_third(1)
    pass_on(SECOND)

    factor = 0.25 * advantage[...].astype(F32)
    for r in range(HEADS):
        block = jnp.transpose(target[:, r * HD : (r + 1) * HD].astype(F32))
        go_t[:, r * rows : (r + 1) * rows] = (block * factor).astype(BF16)

    def queries(s):
        q = finish(s)
        first = PIECES[s][0] // HD
        for i in range(PIECES[s][1] // HD):
            one = q[:, i * HD : (i + 1) * HD]
            q_rows[(first + i) * rows : (first + i + 1) * rows] = one
            q_t[:, (first + i) * rows : (first + i + 1) * rows] = jnp.transpose(one.astype(F32)).astype(BF16)

    queries(FIRST)
    share_last(0)

    blocks = jnp.minimum(c, WINDOW) + 1
    groups = (blocks + GROUP - 1) // GROUP

    def prepare_keys(j, diagonal):
        key_t[:, pl.ds(pl.multiple_of(j * rows, rows), rows)] = (
            jnp.transpose(key_win[j, :rows].astype(F32)).astype(BF16)
        )
        ids = jnp.transpose(key_win[j, rows:].astype(F32))
        for k in range(rows // HD):
            visible = ids[:, k : k + 1] == seg_row
            if diagonal:
                k_pos = lax.broadcasted_iota(jnp.int32, (HD, rows), 0) + k * HD
                q_pos = lax.broadcasted_iota(jnp.int32, (HD, rows), 1)
                visible = visible & (k_pos <= q_pos)
            bias[j, k * HD : (k + 1) * HD] = jnp.where(visible, 0.0, HIDDEN)

    prepare_keys(0, True)

    @pl.loop(1, blocks)
    def _(j):
        prepare_keys(j, False)

    @pl.loop(blocks, groups * GROUP)
    def _(j):
        span = pl.ds(pl.multiple_of(j * rows, rows), rows)
        key_win[j] = jnp.zeros((rows + 16, HD), BF16)
        value_win[j] = jnp.zeros((rows, HD), BF16)
        key_t[:, span] = jnp.zeros((HD, rows), BF16)
        value_t[:, span] = jnp.zeros((HD, rows), BF16)
        bias[j] = jnp.full((rows, rows), HIDDEN, F32)

    def prepare_values():
        for j in (0, 4, 1, 2, 3, 8, 5, 6, 7):
            if j % 4:
                here(1, j)

            def one(j=j):
                value_t[:, j * rows : (j + 1) * rows] = jnp.transpose(value_win[j].astype(F32)).astype(BF16)

            pl.when(c >= j)(one)

    def part(s):
        off, wide = PIECES[s]
        heads = wide // HD
        return off // HD, heads, pl.ds(off // HD * rows, heads * rows), heads * rows

    def score(s):
        _, heads, span, n = part(s)

        def score_group(g, top):
            for u in range(GROUP):
                j = g * GROUP + u
                block = jnp.dot(key_win[j, :rows], q_t[:, span], preferred_element_type=F32)
                block = block + jnp.concatenate([bias[j]] * heads, axis=1)
                scores[j, :, span] = block
                top = jnp.maximum(top, jnp.max(block.reshape(rows // 8, 8, n), 0))
            return top

        top = lax.fori_loop(0, groups, score_group, jnp.full((8, n), HIDDEN, F32))
        return jnp.max(top, 0, keepdims=True) * EXP_SCALE

    def output(s, top):
        first, heads, span, n = part(s)
        out_t[:, :n] = jnp.zeros((HD, n), F32)

        def expo_group(g, total):
            ebs = []
            for u in range(GROUP):
                j = g * GROUP + u
                e = jnp.exp2(scores[j, :, span] * EXP_SCALE - top)
                eb = e.astype(BF16)
                expo[j, :, span] = eb
                ebs.append(eb)
                total = total + jnp.sum(e.reshape(rows // 8, 8, n), 0)
            keys = pl.ds(pl.multiple_of(g * GROUP * rows, rows), GROUP * rows)
            out_t[:, :n] += jnp.dot(
                value_t[:, keys], jnp.concatenate(ebs, axis=0), preferred_element_type=F32
            )
            return total

        total = lax.fori_loop(0, groups, expo_group, jnp.zeros((8, n), F32))
        inverse = 1.0 / jnp.sum(total, 0, keepdims=True)
        out_b = (out_t[:, :n] * inverse).astype(BF16).astype(F32)
        go = go_t[:, span].astype(F32)
        delta = jnp.sum(go * out_b, 0, keepdims=True) * inverse
        scaled = go * inverse
        gp_t[:, span] = scaled.astype(BF16)
        for i in range(heads):
            r = first + i
            attn[:, r * HD : (r + 1) * HD] = jnp.transpose(out_b[:, i * rows : (i + 1) * rows]).astype(BF16)
            gp_rows[r * rows : (r + 1) * rows] = jnp.transpose(scaled[:, i * rows : (i + 1) * rows]).astype(BF16)
        return delta

    def give(w, j, to, when):
        start(remote(
            pair_send.at[w, j], pair_recv.at[w, j], pair_ssem.at[w, j], pair_rsem.at[w, j], ctx=to,
        ), when)

    def take(w, j, into, when):
        def add_in():
            arrived(pair_recv.at[w, j], pair_rsem.at[w, j])
            pair_acc[w, into] += pair_recv[w, j].astype(F32)

        pl.when(when)(add_in)

    def give_sum(w, j):
        def store():
            pair_send[w, j] = pair_acc[w, j].astype(BF16)

        pl.when(c >= j)(store)
        give(w, j, jnp.maximum(c - j, 0), c >= j)

    def keep(w, j, value):
        if j % 4 == 0:
            pair_acc[w, j // 4 * 4] = value
        else:
            pair_send[w, j] = value.astype(BF16)

    def after_group(w, g):
        for j in reversed(range(g * GROUP, (g + 1) * GROUP)):
            if j % 4:
                give(w, j, z * 4 + lax.rem(y + 8 - j, 4), c >= j)

    def pair_second(w):
        for j in (7, 6, 5, 3, 2, 1):
            take(w, j, 4 * ((y + j) // 4), z * 4 + lax.rem(y + j, 4) >= j)
            if j == 5:
                give_sum(w, 8)
        give_sum(w, 4)

    def pair_third(w):
        for j in (8, 4):
            take(w, j, 0, z + j // 4 < rings)

    def backward_values():
        later = part(SECOND)[2]

        def group(g):
            for u in reversed(range(GROUP)):
                j = g * GROUP + u
                dv = jnp.dot(expo[j, :, later], gp_rows[later], preferred_element_type=F32)
                keep(1, j, pair_acc[1, j] + dv)

        for g in reversed(range(WINDOW // GROUP + 1)):
            pl.when(g < groups)(functools.partial(group, g))
            after_group(1, g)

    def score_gradients(s, j, delta):
        _, _, span, _ = part(s)
        dp = jnp.dot(value_win[j], gp_t[:, span], preferred_element_type=F32)
        expo[j, :, span] = (expo[j, :, span].astype(F32) * (dp - delta)).astype(BF16)

    def backward_first(delta):
        sooner = part(FIRST)[2]

        @pl.loop(0, groups)
        def _(g):
            for u in range(GROUP):
                j = g * GROUP + u
                pair_acc[1, j] = jnp.dot(expo[j, :, sooner], gp_rows[sooner], preferred_element_type=F32)
                score_gradients(FIRST, j, delta)

    def backward_keys(delta):
        def group(g):
            for u in reversed(range(GROUP)):
                j = g * GROUP + u
                score_gradients(SECOND, j, delta)
                keep(0, j, jnp.dot(expo[j], q_rows[...], preferred_element_type=F32) * SCALE)

        for g in reversed(range(WINDOW // GROUP + 1)):
            pl.when(g < groups)(functools.partial(group, g))
            after_group(0, g)

    def backward_queries(s):
        first, heads, span, n = part(s)
        dq_t[:, :n] = jnp.zeros((HD, n), F32)

        @pl.loop(0, groups)
        def _(g):
            keys = pl.ds(pl.multiple_of(g * GROUP * rows, rows), GROUP * rows)
            ds = jnp.concatenate([expo[g * GROUP + u, :, span] for u in range(GROUP)], axis=0)
            dq_t[:, :n] += jnp.dot(key_t[:, keys], ds, preferred_element_type=F32)

        inner = jnp.zeros((1, rows), F32)
        for i in range(heads):
            r = first + i
            one = dq_t[:, i * rows : (i + 1) * rows] * SCALE
            dproj[h, :, r * HD : (r + 1) * HD] = jnp.transpose(one).astype(BF16)
            inner += jnp.sum(one * q_t[:, r * rows : (r + 1) * rows].astype(F32), 0, keepdims=True)
        return inner

    def slot(ref, s, who, lo, size):
        off, wide = PIECES[s]
        return ref.at[who, pl.ds(lo, size), pl.ds(off, wide)]

    def move(s, n, who, lo, size, to):
        start(remote(slot(dproj, s, who, lo, size), slot(dproj, s, who, lo, size),
                     ag_send.at[s, n], ag_recv.at[s, n], head=to))

    def landed_piece(s, n, who, lo, size):
        arrived(slot(dproj, s, who, lo, size), ag_recv.at[s, n])

    def gather_send(s):
        for n, to in ((3, partner), (2, far), (0, right), (1, left)):
            if s != SECOND or n != 2:
                move(s, n, h, 0, rows, to)

    def gather_on(s):
        landed_piece(s, 0, left, 0, rows)
        move(s, 2, left, 0, half, right)
        landed_piece(s, 1, right, 0, rows)
        move(s, 7, right, half, half, left)
        move(s, 4, left, 0, rows, partner)
        move(s, 5, right, 0, rows, partner)

    def gather_far(s):
        landed_piece(s, 2, far, 0, half)
        landed_piece(s, 7, far, half, half)
        move(s, 6, far, 0, rows, partner)

    def gather_pass(s):
        for n, who in enumerate((left, right, far)):
            landed_piece(s, n, who, 0, rows)
            move(s, 4 + n, who, 0, rows, partner)

    def add(s, who, fresh=False):
        off, wide = PIECES[s]
        value = lax.dot_general(
            dproj[who, :, off : off + wide], wv[who, :, off : off + wide],
            (((1,), (1,)), ((), ())), preferred_element_type=F32,
        )
        if fresh:
            dnormed[...] = value
        else:
            dnormed[...] += value

    def add_own(s, fresh=False):
        add(s, h, fresh)
        for who in (left, right, far):
            add(s, who)

    def add_rest(s):
        landed_piece(s, 3, partner, 0, rows)
        add(s, partner)
        for n, d in enumerate((3, 1, 2)):
            who = head_of(x + d, 1 - p)
            landed_piece(s, 4 + n, who, 0, rows)
            add(s, who)

    top_first = score(FIRST)
    queries(SECOND)
    top_second = score(SECOND)
    prepare_values()
    delta_first = output(FIRST, top_first)
    backward_first(delta_first)
    inner = backward_queries(FIRST)
    gather_send(FIRST)
    delta_second = output(SECOND, top_second)
    backward_values()
    backward_keys(delta_second)
    inner += backward_queries(SECOND)
    gather_send(SECOND)
    pair_second(1)
    gather_pass(FIRST)
    add_own(FIRST, True)
    pair_second(0)
    gather_on(SECOND)
    pair_third(1)
    dproj[h, :, PIECES[VALUES][0] :] = pair_acc[1, 0].astype(BF16)
    gather_send(VALUES)
    add_rest(FIRST)
    pair_third(0)
    dproj[h, :, PIECES[KEYS][0] : PIECES[VALUES][0]] = pair_acc[0, 0].astype(BF16)
    gather_send(KEYS)
    gather_far(SECOND)
    prod = pair_acc[0, 0] * key_win[0, :rows].astype(F32) + pair_acc[1, 0] * value_win[0].astype(F32)
    inner += jnp.sum(jnp.transpose(prod), 0, keepdims=True)
    inner_stats[0] = jnp.broadcast_to(inner, (8, rows))
    small_first(inner_stats, in_send, in_recv)
    add_own(SECOND)
    add_rest(SECOND)
    gather_pass(VALUES)
    small_second(inner_stats, in_send, in_recv)
    add_own(VALUES)
    add_rest(VALUES)
    gather_pass(KEYS)
    add_own(KEYS)
    inner_col = small_total(inner_stats, in_recv)
    add_rest(KEYS)

    scale = recip[:, :1]
    weighted = tok[...].astype(F32) * scale
    gain_part = jnp.sum(dnormed[...] * weighted, 0, keepdims=True)
    lanes = wide_in // 128
    gain_stats[0] = jnp.zeros((8, 128), F32)
    for k in range(lanes):
        gain_stats[0, k : k + 1] = gain_part[:, k * 128 : (k + 1) * 128]
    before = len(started)
    for d in range(1, n_ctx):
        start(remote(
            gain_stats.at[0], gain_stats.at[d], gg_send.at[d], gg_recv.at[d], ctx=lax.rem(c + d, n_ctx),
        ))
    grad_tokens[...] = (
        dnormed[...] * gain[...].reshape(1, wide_in) * scale - weighted * (scale * inner_col * (1.0 / D))
    ).astype(BF16)
    settle(started[:before])
    gain_total = gain_stats[0]
    for d in range(1, n_ctx):
        arrived(gain_stats.at[d], gg_recv.at[d])
        gain_total = gain_total + gain_stats[d]
    grad_gain[...] = gain_total

    settle(started[before:])


def hand_over(attn, grad_tokens, gain_rows, attn_out, grad_out, gain_out):
    attn_out[...] = attn[...]
    grad_out[...] = grad_tokens[...]
    wide = gain_out.shape[0]
    gain_out[...] = gain_rows[: wide // 128].reshape(wide)


def on_device(n_ctx, tokens, gain, qkv_weight, target, advantage, segment):
    rows, wide = tokens.shape
    group = qkv_weight.shape[1] // 8
    n = 3 * rows
    every = HEADS * rows
    slots = WINDOW + 1
    vmem = pl.BlockSpec(memory_space=pltpu.VMEM)
    anywhere = pl.BlockSpec(memory_space=pl.ANY)
    scratch = [
        ((rows, wide), BF16), ((8, wide, group), BF16),
        ((4, rows, group), BF16), ((4, rows, group), BF16), ((3, rows, group), BF16),
        ((2, rows // 2, group), F32), ((rows, group), F32),
        ((2, rows // 2, group), BF16), ((2, rows, group), BF16), ((2, rows, HD), BF16),
        ((6, 8, rows), F32), ((rows, HD), F32),
        ((slots, rows + 16, HD), BF16), ((slots, rows, HD), BF16),
        ((HD, slots * rows), BF16), ((HD, slots * rows), BF16), ((slots, rows, rows), F32),
        ((HEADS * rows, HD), BF16), ((HD, HEADS * rows), BF16), ((HD, HEADS * rows), BF16),
        ((slots, rows, every), F32), ((slots, rows, every), BF16), ((HD, n), F32),
        ((every, HD), BF16), ((HD, every), BF16), ((HD, n), F32),
        ((2, slots, rows, HD), F32), ((2, slots, rows, HD), BF16), ((2, slots, rows, HD), BF16),
        ((8, rows, group), BF16), ((6, 8, rows), F32), ((rows, wide), F32), ((n_ctx, 8, 128), F32),
    ]
    sems = [
        (4, 8), (4, 4), (4, 4), (4, 2), (4, 2), (4, 4), (4, 4), (4,), (4,),
        (2, 12), (2, slots), (2, slots), (2, slots),
        (4, 8), (4, 8), (4,), (4,), (n_ctx,), (n_ctx,),
    ]
    out_types = (
        jax.ShapeDtypeStruct((rows, HEADS * HD), BF16),
        jax.ShapeDtypeStruct((rows, wide), BF16),
    )
    out, grad_tokens, gain_rows = pl.pallas_call(
        functools.partial(kernel, n_ctx),
        out_shape=(*out_types, jax.ShapeDtypeStruct((8, 128), F32)),
        in_specs=[vmem, vmem, anywhere, vmem, vmem, vmem],
        out_specs=(vmem, vmem, vmem),
        scratch_shapes=[pltpu.VMEM(shape, dtype) for shape, dtype in scratch]
        + [pltpu.SemaphoreType.DMA(shape) for shape in sems],
        compiler_params=pltpu.CompilerParams(
            collective_id=0, has_side_effects=True, vmem_limit_bytes=60 * 1024 * 1024
        ),
    )(
        tokens, gain, qkv_weight, target,
        advantage.reshape(1, rows), segment.reshape(1, rows),
    )
    return pl.pallas_call(
        hand_over,
        out_shape=(*out_types, jax.ShapeDtypeStruct((wide,), F32)),
        in_specs=[vmem, vmem, vmem],
        out_specs=(vmem, vmem, vmem),
    )(out, grad_tokens, gain_rows)


def solution(mesh):
    placed = (P("ctx", "head"), P("head"), P("head", None), P("ctx", "head"), P("ctx"), P("ctx"))
    return jax.shard_map(
        functools.partial(on_device, mesh.shape["ctx"]),
        mesh=mesh,
        in_specs=placed,
        out_specs=(P("ctx", "head"), P("ctx", "head"), P("head")),
        check_vma=False,
    )
```
